256 devices in a mesh: ep: 64 (over x, z, core), cp: 4 (over y).
Axes of the slice: x: 4, y: 4, z: 8, core: 2. Of those that a mesh axis runs over, the one named last changes fastest.
Arguments:
- grad_out: bfloat16 [32768, 4096], P('ep', 'cp'), may hold values from -6 to 6
- route_ids: int32 [32768, 4], P('ep'), may hold values from 0 to 63, as said below
- fallback_ids: int32 [32768, 4], P('ep'), may hold values from 0 to 63
- slot_ids: int32 [32768, 4], P('ep'), may hold values from 0 to 79, as said below
- route_probs: float32 [32768, 4], P('ep'), may hold values from 0.05 to 0.5
- w_gate: bfloat16 [64, 768, 4096], P('ep', None, 'cp'), may hold values from -0.09375 to 0.09375
- w_up: bfloat16 [64, 768, 4096], P('ep', None, 'cp'), may hold values from -0.09375 to 0.09375
- w_down: bfloat16 [64, 768, 4096], P('ep', None, 'cp'), may hold values from -0.21875 to 0.21875
- gate_pre: bfloat16 [64, 768, 2560], P('ep', 'cp'), may hold values from -5 to 5
- up_pre: bfloat16 [64, 768, 2560], P('ep', 'cp'), may hold values from -5 to 5
- queries: bfloat16 [32768, 4096], P(('ep', 'cp')), may hold values from -5 to 5
- key_vectors: bfloat16 [32768, 256], P('ep'), may hold values from -5 to 5
- value_vectors: bfloat16 [32768, 256], P('ep'), may hold values from -6 to 6
- block_mask: int32 [64, 8, 8], P('ep'), may hold values 0 or 1
Outputs:
- grad_hidden: bfloat16 [32768, 4096], P(('ep', 'cp'))
- grad_queries: bfloat16 [32768, 4096], P(('ep', 'cp'))
- grad_keys: bfloat16 [32768, 256], P(('ep', 'cp'))
- grad_values: bfloat16 [32768, 256], P(('ep', 'cp'))
The draws below stay inside these ranges and needn't reach their ends.
Inputs may be any that keep to these rules, and one draw needn't show every extreme that they name: `route_ids`: each row names 4 different experts. `slot_ids`: a value below 40 is a slot at the route's expert in route_ids, a value of 40 or more is 40 plus a slot at its expert in fallback_ids; within one sequence shard no two routes take the same slot of the same expert.
All inputs are finite; a program needn't handle non-finite values. No bound on the sum of `block_mask` on one device may be relied on, other than what follows from the above.
Results may differ from the reference program's by a relative error of at most 0.034.
Values may be sent and summed in bfloat16 or wider, within the bound.
No kernel may reach another device: no remote copies, remote signals or barrier semaphores. Data moves between devices by JAX's collectives and lax.ppermute only.
A program may use at most 128 MiB of HBM per device.

```python
import math
from functools import partial
import jax
import jax.numpy as jnp
from jax import lax

D = 4096
HID = 768
HEADS = 32
KV_HEADS = 2
HEAD_DIM = 128
TOPK = 4
SHARD = 512
EXPERTS = 64
CAP = 40
TOKENS = 32768
BLOCK = 64
NBLK = 8
N_EP = 64
N_CP = 4


def shard_routes(shard_key, boost_table):
    score_key, order_key, spare_key = jax.random.split(shard_key, 3)
    scores = jax.random.randint(score_key, (SHARD, EXPERTS), 0, 1000) + boost_table[None, :]
    scores = scores * EXPERTS + jnp.arange(EXPERTS, dtype=jnp.int32)[None, :]
    primary = lax.top_k(scores, TOPK)[1].astype(jnp.int32).reshape(-1)
    onehot_table = (primary[:, None] == jnp.arange(EXPERTS, dtype=jnp.int32)[None, :]).astype(jnp.int32)
    earlier = jnp.cumsum(onehot_table, axis=0) - onehot_table
    rank_in = jnp.sum(earlier * onehot_table, axis=1)
    demand = jnp.sum(onehot_table, axis=0)
    kept_count = jnp.minimum(demand, CAP)
    spilled = (rank_in >= CAP).astype(jnp.int32)
    spill_rank = jnp.cumsum(spilled) - spilled
    expert_order = jax.random.permutation(order_key, EXPERTS).astype(jnp.int32)
    free_cells = (jnp.arange(CAP, dtype=jnp.int32)[None, :] >= kept_count[expert_order][:, None]).astype(jnp.int32).reshape(-1)
    free_count = jnp.cumsum(free_cells)
    position = jnp.minimum(jnp.searchsorted(free_count, spill_rank + 1), EXPERTS * CAP - 1).astype(jnp.int32)
    spare_ids = jax.random.randint(spare_key, primary.shape, 0, EXPERTS).astype(jnp.int32)
    fallback = jnp.where(spilled > 0, expert_order[position // CAP], spare_ids)
    slot_out = jnp.where(spilled > 0, position % CAP + CAP, rank_in)
    return (primary.reshape(SHARD, TOPK), fallback.reshape(SHARD, TOPK).astype(jnp.int32), slot_out.reshape(SHARD, TOPK).astype(jnp.int32))


def route_table(key):
    hot_order = jax.random.permutation(jax.random.fold_in(key, 101), EXPERTS)
    boost_table = jnp.zeros((EXPERTS,), jnp.int32).at[hot_order[:3]].set(jnp.array([320, 220, 140], jnp.int32))
    shard_keys = jax.random.split(jax.random.fold_in(key, 102), TOKENS // SHARD)
    primary, fallback, slot_out = jax.vmap(partial(shard_routes, boost_table=boost_table))(shard_keys)
    return (primary.reshape(TOKENS, TOPK), fallback.reshape(TOKENS, TOPK), slot_out.reshape(TOKENS, TOPK))


def draw_route_ids(key, part):
    return route_table(key)[0]


def draw_fallback_ids(key, part):
    return route_table(key)[1]


def draw_slot_ids(key, part):
    return route_table(key)[2]


def draw_queries(key, part):
    key = jax.random.fold_in(key, 11)
    return jnp.clip(jax.random.normal(key, (TOKENS, HEADS * HEAD_DIM), jnp.float32), -5.0, 5.0).astype(jnp.bfloat16)


def draw_key_vectors(key, part):
    key = jax.random.fold_in(key, 12)
    return jnp.clip(jax.random.normal(key, (TOKENS, KV_HEADS * HEAD_DIM), jnp.float32), -5.0, 5.0).astype(jnp.bfloat16)


def set_ends(values, key, least, largest):
    place = [jax.random.randint(jax.random.fold_in(key, axis), (), 0, length) for axis, length in enumerate(values.shape)]
    main_axis = values.shape.index(max(values.shape))
    next_to = place[:main_axis] + [(place[main_axis] + 1) % values.shape[main_axis]] + place[main_axis + 1:]
    return values.at[tuple(place)].set(least).at[tuple(next_to)].set(largest)


def steps_of(own_key, extent, cuts, low, top_value):
    factor_of = 1.0
    for dim, blocks in cuts:
        steps = jax.random.uniform(jax.random.fold_in(jax.random.fold_in(own_key, 6), dim), (blocks,), jnp.float32, low / len(cuts), top_value / len(cuts))
        factor_of = factor_of * jnp.repeat(jnp.exp(steps), extent[dim] // blocks).reshape((-1,) + (1,) * (len(extent) - 1 - dim))
    return factor_of


def bell_draw(rng, extent, spread, reach, cuts=(), held_as=jnp.bfloat16):
    drawn = jax.random.normal(rng, extent, jnp.float32) * spread
    if len(cuts) > 0:
        drawn = steps_of(rng, extent, cuts, -0.22, 0.18) * drawn
    return jnp.clip(drawn, min=-reach, max=reach).astype(held_as)


def setup_inputs(seed: int = 0) -> dict:
    key_of = jax.random.split(jax.random.key(seed), 15)
    return {
        "grad_out": bell_draw(key_of[0], (TOKENS, D), 1.0, 6.0, ((0, 64), (1, 4))),
        "route_ids": draw_route_ids(jax.random.fold_in(key_of[14], 71), 0),
        "fallback_ids": draw_fallback_ids(jax.random.fold_in(key_of[14], 71), 0),
        "slot_ids": draw_slot_ids(jax.random.fold_in(key_of[14], 71), 0),
        "route_probs": jnp.clip(jnp.exp(math.log(0.5) - 2.3025851 * jax.random.uniform(key_of[4], (TOKENS, TOPK), jnp.float32) ** steps_of(key_of[4], (TOKENS, TOPK), ((0, 64),), -0.2, 0.2)), 0.05, 0.5),
        "w_gate": bell_draw(key_of[5], (EXPERTS, HID, D), D ** -0.5, 0.09375, ((0, 64), (2, 4))),
        "w_up": bell_draw(key_of[6], (EXPERTS, HID, D), D ** -0.5, 0.09375, ((0, 64), (2, 4))),
        "w_down": bell_draw(key_of[7], (EXPERTS, HID, D), HID ** -0.5, 0.21875, ((0, 64), (2, 4))),
        "gate_pre": bell_draw(key_of[8], (EXPERTS, HID, EXPERTS * CAP), 1.0, 5.0, ((0, 64), (1, 4))),
        "up_pre": bell_draw(key_of[9], (EXPERTS, HID, EXPERTS * CAP), 1.0, 5.0, ((0, 64), (1, 4))),
        "queries": draw_queries(jax.random.fold_in(key_of[14], 71), 0),
        "key_vectors": draw_key_vectors(jax.random.fold_in(key_of[14], 71), 0),
        "value_vectors": bell_draw(key_of[12], (TOKENS, KV_HEADS * HEAD_DIM), 1.0, 6.0, ((0, 64),)),
        "block_mask": set_ends((jax.random.randint(key_of[13], (N_EP, NBLK, NBLK), 0, 3) < 2).astype(jnp.int32), jax.random.fold_in(key_of[13], 1), 0, 1),
    }


def silu_grads(hidden_grad, gate_saved, up_saved):
    gate_value = gate_saved.astype(jnp.float32)
    up_value = up_saved.astype(jnp.float32)
    sigmoid_gate = jax.nn.sigmoid(gate_value)
    gate_grad = hidden_grad * up_value * sigmoid_gate * (1.0 + gate_value * (1.0 - sigmoid_gate))
    up_grad = hidden_grad * gate_value * sigmoid_gate
    return gate_grad.astype(jnp.bfloat16), up_grad.astype(jnp.bfloat16)


def attend_window(queries, key_vectors, value_vectors, out_grad, mask_table):
    length = queries.shape[0]
    group_size = HEADS // KV_HEADS
    score_scale = HEAD_DIM ** -0.5
    query_heads = queries.astype(jnp.float32).reshape(length, KV_HEADS, group_size, HEAD_DIM)
    grad_heads = out_grad.astype(jnp.float32).reshape(length, KV_HEADS, group_size, HEAD_DIM)
    key_heads = key_vectors.astype(jnp.float32).reshape(length, KV_HEADS, HEAD_DIM)
    value_heads = value_vectors.astype(jnp.float32).reshape(length, KV_HEADS, HEAD_DIM)
    position = jnp.arange(length, dtype=jnp.int32)
    block_index = position // BLOCK
    near_block = mask_table[block_index][:, block_index] > 0
    same_block = block_index[:, None] == block_index[None, :]
    visible = (position[None, :] <= position[:, None]) & (same_block | near_block)
    scores = jnp.einsum("qhgd,khd->hgqk", query_heads, key_heads) * score_scale
    scores = jnp.where(visible, scores, -jnp.inf)
    row_peak = jnp.max(scores, axis=-1, keepdims=True)
    exponent = jnp.exp(scores - row_peak)
    prob_rows = exponent / jnp.sum(exponent, axis=-1, keepdims=True)
    probs_low = lax.optimization_barrier(prob_rows.astype(jnp.bfloat16)).astype(jnp.float32)
    prob_grad = jnp.einsum("qhgd,khd->hgqk", grad_heads, value_heads)
    row_total = jnp.sum(prob_rows * prob_grad, axis=-1, keepdims=True)
    score_grad = lax.optimization_barrier((prob_rows * (prob_grad - row_total)).astype(jnp.bfloat16)).astype(jnp.float32)
    grad_query = (jnp.einsum("hgqk,khd->qhgd", score_grad, key_heads) * score_scale).astype(jnp.bfloat16)
    grad_key = (jnp.einsum("hgqk,qhgd->khd", score_grad, query_heads) * score_scale).astype(jnp.bfloat16)
    grad_value = jnp.einsum("hgqk,qhgd->khd", probs_low, grad_heads).astype(jnp.bfloat16)
    return grad_query.reshape(length, -1), grad_key.reshape(length, -1), grad_value.reshape(length, -1)


def reference(grad_out, route_ids, fallback_ids, slot_ids, route_probs, w_gate, w_up, w_down, gate_pre, up_pre, queries, key_vectors, value_vectors, block_mask):
    slot_count = EXPERTS * CAP
    route_count = TOKENS * TOPK
    overflow = slot_ids >= CAP
    target = jnp.where(overflow, fallback_ids, route_ids).reshape(-1)
    slot_local = jnp.where(overflow, slot_ids - CAP, slot_ids).reshape(-1)
    route_index = jnp.arange(route_count, dtype=jnp.int32)
    token_index = route_index // TOPK
    buffer_row = target * slot_count + (token_index // SHARD) * CAP + slot_local
    owners = jnp.full((EXPERTS * slot_count,), -1, jnp.int32).at[buffer_row].set(route_index)
    owners = owners.reshape(EXPERTS, slot_count)
    prob_flat = route_probs.reshape(-1)
    quarter = D // N_CP

    def one_expert(moe_total, inputs):
        expert_owners, gate_rows, up_rows, down_rows, gate_saved, up_saved = inputs
        filled = expert_owners >= 0
        source_route = jnp.maximum(expert_owners, 0)
        source_token = source_route // TOPK
        weight = jnp.where(filled, prob_flat[source_route], 0.0)
        routed = (grad_out[source_token].astype(jnp.float32) * weight[:, None]).astype(jnp.bfloat16)
        hidden_grad = jnp.zeros((HID, slot_count), jnp.float32)
        for group_index in range(N_CP):
            column_start = group_index * quarter
            partial_sum = jnp.dot(down_rows[:, column_start:column_start + quarter], routed[:, column_start:column_start + quarter].T, preferred_element_type=jnp.float32)
            hidden_grad = hidden_grad + lax.optimization_barrier(partial_sum.astype(jnp.bfloat16)).astype(jnp.float32)
        gate_grad, up_grad = silu_grads(hidden_grad, gate_saved, up_saved)
        expert_grad = jnp.dot(gate_grad.T, gate_rows, preferred_element_type=jnp.float32) + jnp.dot(up_grad.T, up_rows, preferred_element_type=jnp.float32)
        expert_grad = lax.optimization_barrier(expert_grad.astype(jnp.bfloat16)).astype(jnp.float32)
        expert_grad = jnp.where(filled[:, None], expert_grad, 0.0)
        return moe_total.at[source_token].add(expert_grad), None

    moe_total = lax.scan(one_expert, jnp.zeros((TOKENS, D), jnp.float32), (owners, w_gate, w_up, w_down, gate_pre, up_pre))[0]
    grad_hidden = (grad_out.astype(jnp.float32) + moe_total).astype(jnp.bfloat16)
    shards = TOKENS // SHARD

    def one_window(inputs):
        return attend_window(inputs[0], inputs[1], inputs[2], inputs[3], inputs[4])

    grad_queries, grad_keys, grad_values = lax.map(one_window, (queries.reshape(shards, SHARD, -1), key_vectors.reshape(shards, SHARD, -1), value_vectors.reshape(shards, SHARD, -1), grad_hidden.reshape(shards, SHARD, D), block_mask))
    return grad_hidden, grad_queries.reshape(TOKENS, -1), grad_keys.reshape(TOKENS, -1), grad_values.reshape(TOKENS, -1)
```

```python
import functools

import jax
import jax.numpy as jnp
from jax import lax
from jax.experimental import pallas as pl
from jax.experimental.pallas import tpu as pltpu
from jax.sharding import PartitionSpec as P

HEAD_DIM = 128
LANES = 128
PARTS = 2
STEPS = 4
VMEM_LIMIT = 60 * 1024 * 1024

f32 = jnp.float32
bf16 = jnp.bfloat16


def params():
    return pltpu.CompilerParams(vmem_limit_bytes=VMEM_LIMIT)


def cost(flops, moved, exps=0):
    return pl.CostEstimate(flops=flops, bytes_accessed=moved, transcendentals=exps)


def weave(out_ref, wide, low, high):
    rows = low.shape[0]
    for j in range(wide.shape[0]):
        cols = slice(j * LANES, (j + 1) * LANES)
        wide[j, pl.ds(0, rows, 2), :] = low[:, cols]
        wide[j, pl.ds(1, rows, 2), :] = high[:, cols]
        out_ref[:, cols] = wide[j].astype(bf16)


def unweave(rows_ref, wide):
    slabs, rows = wide.shape[0], wide.shape[1] // 2
    for j in range(slabs):
        wide[j] = rows_ref[:, j * LANES : (j + 1) * LANES].astype(f32)
    low = [wide[j, pl.ds(0, rows, 2), :].astype(bf16) for j in range(slabs)]
    high = [wide[j, pl.ds(1, rows, 2), :].astype(bf16) for j in range(slabs)]
    return jnp.concatenate(low, axis=1), jnp.concatenate(high, axis=1)


def woven(rows, half):
    return pltpu.VMEM((half // LANES, 2 * rows, LANES), f32)


def split_by(row, size, count):
    factor = (1 << 16) // size + 1
    assert all((r * factor) >> 16 == r // size for r in range(count))
    return (row * factor) >> 16


def route_rows(part, capacity, ids_ref, spare_ref, slot_ref, probs_ref, grad_ref, out_ref, wide):
    rows, half = out_ref.shape[0] // 2, out_ref.shape[1]
    tokens = grad_ref.shape[0]
    share = capacity // PARTS
    overflow = slot_ref[...] >= capacity
    expert = jnp.where(overflow, spare_ref[...], ids_ref[...])
    target = expert * capacity + slot_ref[...] - jnp.where(overflow, capacity, 0)
    row = lax.broadcasted_iota(jnp.int32, (rows, 1), 0) + pl.program_id(0) * rows
    group = split_by(row, share, rows * STEPS)
    dest = group * (capacity - share) + row + part * share
    weights = jnp.zeros((rows, tokens), f32)
    for k in range(target.shape[0]):
        weights = jnp.where(target[k : k + 1, :] == dest, probs_ref[k : k + 1, :], weights)
    weight = jnp.sum(weights, axis=1, keepdims=True)
    chosen = jnp.where(weights != 0.0, 1.0, 0.0).astype(bf16)
    picked = jnp.dot(chosen, grad_ref[...], preferred_element_type=f32)
    picked = picked * weight
    weave(out_ref, wide, picked[:, :half], picked[:, half:])


def send_rows(part, experts, capacity, ids, spare, slots, probs, grad):
    rows, (tokens, width) = experts * capacity // PARTS, grad.shape
    step, half = rows // STEPS, width // 2
    routes = pl.BlockSpec(slots.shape, lambda i: (0, 0))
    return pl.pallas_call(
        functools.partial(route_rows, part, capacity),
        grid=(STEPS,),
        in_specs=[routes] * 4 + [pl.BlockSpec(grad.shape, lambda i: (0, 0))],
        out_specs=pl.BlockSpec((2 * step, half), lambda i: (i, 0)),
        out_shape=jax.ShapeDtypeStruct((2 * rows, half), bf16),
        scratch_shapes=[woven(step, half)],
        compiler_params=params(),
        cost_estimate=cost(2 * rows * tokens * width, 4 * rows * width),
        name="send_rows",
    )(ids, spare, slots, probs, grad)


def turn_kernel(share, saved_ref, *refs):
    outs, tall = refs[:-1], refs[-1]
    quarters, kinds = saved_ref.shape[:2]
    groups = saved_ref.shape[3] // (PARTS * share)
    for kind in range(kinds):
        hidden = jnp.concatenate([saved_ref[c, kind] for c in range(quarters)], axis=0)
        rows = hidden.astype(f32).T
        for part in range(PARTS):
            for g in range(groups):
                start = (g * PARTS + part) * share
                tall[g * share : (g + 1) * share, :] = rows[start : start + share, :]
            outs[part * kinds + kind][...] = tall[...].astype(bf16)


def turn_saved(saved, share):
    quarters, kinds, units, slots = saved.shape
    hidden, rows = quarters * units, slots // PARTS
    step = rows // STEPS
    return pl.pallas_call(
        functools.partial(turn_kernel, share),
        grid=(STEPS,),
        in_specs=[pl.BlockSpec((quarters, kinds, units, PARTS * step), lambda i: (0, 0, 0, i))],
        out_specs=[pl.BlockSpec((step, hidden), lambda i: (i, 0))] * (PARTS * kinds),
        out_shape=[jax.ShapeDtypeStruct((rows, hidden), bf16)] * (PARTS * kinds),
        scratch_shapes=[pltpu.VMEM((step, hidden), f32)],
        compiler_params=params(),
        cost_estimate=cost(saved.size, 4 * saved.size),
        name="turn_saved",
    )(saved)


def down_rows_kernel(rows_ref, down_ref, out_ref, wide):
    half = rows_ref.shape[1]
    low, high = unweave(rows_ref, wide)
    total = jnp.dot(low, down_ref[:half, :], preferred_element_type=f32)
    total = total + jnp.dot(high, down_ref[half:, :], preferred_element_type=f32)
    out_ref[...] = total.astype(bf16)


def project_down(arrived, down_t):
    rows, half = arrived.shape[0] // 2, arrived.shape[1]
    width, hidden = down_t.shape
    step = rows // STEPS
    return pl.pallas_call(
        down_rows_kernel,
        grid=(STEPS,),
        in_specs=[
            pl.BlockSpec((2 * step, half), lambda i: (i, 0)),
            pl.BlockSpec(down_t.shape, lambda i: (0, 0)),
        ],
        out_specs=pl.BlockSpec((step, hidden), lambda i: (i, 0)),
        out_shape=jax.ShapeDtypeStruct((rows, hidden), bf16),
        scratch_shapes=[woven(step, half)],
        compiler_params=params(),
        cost_estimate=cost(2 * rows * width * hidden, 2 * rows * (width + hidden)),
        name="project_down",
    )(arrived, down_t)


def expert_kernel(hidden_ref, gate_ref, up_ref, wg_ref, wu_ref, out_ref, wide):
    rows, half = hidden_ref.shape[0], out_ref.shape[1]
    grad = hidden_ref[...].astype(f32)
    gate = gate_ref[...].astype(f32)
    up = up_ref[...].astype(f32)
    sig = 1.0 / (1.0 + jnp.exp(-gate))
    shared = grad * sig
    gate_grad = (shared * up * (1.0 + gate * (1.0 - sig))).astype(bf16)
    up_grad = (shared * gate).astype(bf16)
    total = jnp.dot(gate_grad, wg_ref[...], preferred_element_type=f32)
    total = total + jnp.dot(up_grad, wu_ref[...], preferred_element_type=f32)
    weave(out_ref, wide, total[:, :half], total[:, half:])


def expert_rows(hidden_grad, gate, up, w_gate, w_up):
    rows, hidden = hidden_grad.shape
    width = w_gate.shape[1]
    step, half = rows // STEPS, width // 2
    row_block = pl.BlockSpec((step, hidden), lambda i: (i, 0))
    whole = pl.BlockSpec(w_gate.shape, lambda i: (0, 0))
    return pl.pallas_call(
        expert_kernel,
        grid=(STEPS,),
        in_specs=[row_block, row_block, row_block, whole, whole],
        out_specs=pl.BlockSpec((2 * step, half), lambda i: (i, 0)),
        out_shape=jax.ShapeDtypeStruct((2 * rows, half), bf16),
        scratch_shapes=[woven(step, half)],
        compiler_params=params(),
        cost_estimate=cost(
            128 * rows * hidden * width, 2 * rows * (3 * hidden + width), rows * hidden
        ),
        name="expert_rows",
    )(hidden_grad, gate, up, w_gate, w_up)


def collect_kernel(slots_ref, rows_ref, base_ref, out_ref, total, wide):
    step = pl.program_id(0)
    tokens = slots_ref.shape[0]
    rows, half = rows_ref.shape[0] // 2, rows_ref.shape[1]

    @pl.when(step == 0)
    def _():
        total[...] = base_ref[...].astype(f32)

    row = lax.broadcasted_iota(jnp.int32, (tokens, rows), 1) + step * rows
    chosen = jnp.zeros((tokens, rows), f32)
    for k in range(slots_ref.shape[1]):
        chosen = jnp.where(slots_ref[:, k : k + 1] == row, 1.0, chosen)
    chosen = chosen.astype(bf16)
    low, high = unweave(rows_ref, wide)
    total[:, :half] += jnp.dot(chosen, low, preferred_element_type=f32)
    total[:, half:] += jnp.dot(chosen, high, preferred_element_type=f32)

    @pl.when(step == STEPS - 1)
    def _():
        out_ref[...] = total[...].astype(out_ref.dtype)


def collect_rows(slots, returned, base, out_dtype):
    tokens, width = base.shape
    rows, half = returned.shape[0] // 2, returned.shape[1]
    step = rows // STEPS
    return pl.pallas_call(
        collect_kernel,
        grid=(STEPS,),
        in_specs=[
            pl.BlockSpec(slots.shape, lambda i: (0, 0)),
            pl.BlockSpec((2 * step, half), lambda i: (i, 0)),
            pl.BlockSpec(base.shape, lambda i: (0, 0)),
        ],
        out_specs=pl.BlockSpec(base.shape, lambda i: (0, 0)),
        out_shape=jax.ShapeDtypeStruct(base.shape, out_dtype),
        scratch_shapes=[pltpu.VMEM((tokens, width), f32), woven(step, half)],
        compiler_params=params(),
        cost_estimate=cost(2 * rows * tokens * width, 2 * rows * width + 8 * tokens * width),
        name="collect_rows",
    )(slots, returned, base)


def probs_kernel(q_ref, k_ref, seen_ref, out_ref):
    length = q_ref.shape[0]
    block = length // 2
    scale = HEAD_DIM ** (-0.5)
    for part in range(2):
        keys = (part + 1) * block
        cols = slice(part * block, (part + 1) * block)
        scores = lax.dot_general(
            k_ref[:keys, :], q_ref[cols, :], (((1,), (1,)), ((), ())), preferred_element_type=f32
        )
        scores = jnp.where(seen_ref[:keys, cols] > 0, scores * scale, -jnp.inf)
        peak = jnp.max(scores, axis=0, keepdims=True)
        exponent = jnp.exp(scores - peak)
        out_ref[0, :keys, cols] = exponent / jnp.sum(exponent, axis=0, keepdims=True)
        if keys < length:
            out_ref[0, keys:, cols] = jnp.zeros((length - keys, block), f32)


def attention_probs(queries, keys, seen):
    length, heads = queries.shape[0], queries.shape[1] // HEAD_DIM
    return pl.pallas_call(
        probs_kernel,
        grid=(heads,),
        in_specs=[
            pl.BlockSpec((length, HEAD_DIM), lambda h: (0, h)),
            pl.BlockSpec(keys.shape, lambda h: (0, 0)),
            pl.BlockSpec(seen.shape, lambda h: (0, 0)),
        ],
        out_specs=pl.BlockSpec((1, length, length), lambda h: (h, 0, 0)),
        out_shape=jax.ShapeDtypeStruct((heads, length, length), f32),
        compiler_params=params(),
        cost_estimate=cost(
            2 * heads * length * length * HEAD_DIM,
            4 * heads * length * length,
            heads * length * length,
        ),
        name="attention_probs",
    )(queries, keys, seen)


def grads_kernel(heads, probs_ref, grad_ref, q_ref, v_ref, kt_ref, out_ref, sum_k, sum_v):
    head = pl.program_id(0)
    length = q_ref.shape[0]
    block = length // 2
    scale = HEAD_DIM ** (-0.5)

    @pl.when(head == 0)
    def _():
        sum_k[...] = jnp.zeros_like(sum_k)
        sum_v[...] = jnp.zeros_like(sum_v)

    @pl.when(head < heads)
    def _():
        for part in range(2):
            keys = (part + 1) * block
            cols = slice(part * block, (part + 1) * block)
            probs = probs_ref[0, :keys, cols]
            grad = grad_ref[cols, :]
            prob_grad = lax.dot_general(
                v_ref[:keys, :], grad, (((1,), (1,)), ((), ())), preferred_element_type=f32
            )
            row_total = jnp.sum(probs * prob_grad, axis=0, keepdims=True)
            score_grad = (probs * (prob_grad - row_total)).astype(bf16)
            query_grad = jnp.dot(kt_ref[:, :keys], score_grad, preferred_element_type=f32) * scale
            out_ref[cols, :] = query_grad.T.astype(bf16)
            sum_k[:keys, :] += jnp.dot(score_grad, q_ref[cols, :], preferred_element_type=f32)
            sum_v[:keys, :] += jnp.dot(probs.astype(bf16), grad, preferred_element_type=f32)

    @pl.when(head == heads)
    def _():
        out_ref[...] = (sum_k[...] * scale).astype(bf16)

    @pl.when(head == heads + 1)
    def _():
        out_ref[...] = sum_v[...].astype(bf16)


def attention_grads(probs, out_grad, queries, values, keys_t):
    heads, length, _ = probs.shape
    head_cols = pl.BlockSpec((length, HEAD_DIM), lambda h: (0, jnp.minimum(h, heads - 1)))
    return pl.pallas_call(
        functools.partial(grads_kernel, heads),
        grid=(heads + 2,),
        in_specs=[
            pl.BlockSpec((1, length, length), lambda h: (jnp.minimum(h, heads - 1), 0, 0)),
            head_cols,
            head_cols,
            pl.BlockSpec((length, HEAD_DIM), lambda h: (0, 0)),
            pl.BlockSpec(keys_t.shape, lambda h: (0, 0)),
        ],
        out_specs=pl.BlockSpec((length, HEAD_DIM), lambda h: (0, h)),
        out_shape=jax.ShapeDtypeStruct((length, (heads + 2) * HEAD_DIM), bf16),
        scratch_shapes=[pltpu.VMEM((length, HEAD_DIM), f32), pltpu.VMEM((length, HEAD_DIM), f32)],
        compiler_params=params(),
        cost_estimate=cost(8 * heads * length * length * HEAD_DIM, 4 * heads * length * length),
        name="attention_grads",
    )(probs, out_grad, queries, values, keys_t)


def to_rows(grads):
    parts = lax.axis_size("cp")
    me = lax.axis_index("cp")
    rows, width = grads.shape[0] // parts, grads.shape[1]
    out = jnp.zeros((rows, parts * width), grads.dtype)
    for shift in range(parts):
        piece = lax.dynamic_slice_in_dim(grads, ((me + shift) % parts) * rows, rows, 0)
        if shift:
            piece = lax.ppermute(piece, "cp", [(i, (i + shift) % parts) for i in range(parts)])
        out = lax.dynamic_update_slice(out, piece, (0, ((me - shift) % parts) * width))
    return out


def to_heads(queries):
    parts = lax.axis_size("cp")
    me = lax.axis_index("cp")
    rows, width = queries.shape[0], queries.shape[1] // parts
    out = jnp.zeros((parts, rows, width), queries.dtype)
    for shift in range(parts):
        piece = lax.dynamic_slice_in_dim(queries, ((me + shift) % parts) * width, width, 1)
        if shift:
            piece = lax.ppermute(piece, "cp", [(i, (i + shift) % parts) for i in range(parts)])
        out = lax.dynamic_update_slice(out, piece[None], ((me - shift) % parts, 0, 0))
    return out.reshape(parts * rows, width)


def seen_keys(mask_table, length):
    blocks = mask_table.shape[0]
    size = length // blocks
    pos = jnp.arange(length, dtype=jnp.int32)
    near = jnp.broadcast_to(mask_table.T[:, None, :, None], (blocks, size, blocks, size))
    near = near.reshape(length, length) > 0
    same = (pos // size)[:, None] == (pos // size)[None, :]
    return ((pos[:, None] <= pos[None, :]) & (same | near)).astype(f32)


def swap(rows, axis):
    return lax.all_to_all(rows, axis, split_axis=0, concat_axis=0, tiled=True)


def on_device(
    grad_out,
    route_ids,
    fallback_ids,
    slot_ids,
    route_probs,
    w_gate,
    w_up,
    w_down,
    gate_pre,
    up_pre,
    queries,
    key_vectors,
    value_vectors,
    block_mask,
):
    experts = lax.axis_size("ep")
    quarters = lax.axis_size("cp")
    tokens, width = grad_out.shape
    slot_count = gate_pre.shape[2]
    capacity = slot_count // experts
    share = capacity // PARTS
    part_rows = experts * share
    half = width // 2

    routes = (route_ids.T, fallback_ids.T, slot_ids.T)
    probs_t = route_probs.T
    outgoing = [
        send_rows(part, experts, capacity, *routes, probs_t, grad_out) for part in range(PARTS)
    ]
    saved = lax.all_gather(jnp.stack([gate_pre[0], up_pre[0]]), "cp", axis=0)

    overflow = routes[2] >= capacity
    expert = jnp.where(overflow, routes[1], routes[0])
    slot = routes[2] - jnp.where(overflow, capacity, 0)
    in_part = [
        jnp.where(slot // share == part, expert * share + slot - part * share, -1).T
        for part in range(PARTS)
    ]
    my_queries = to_heads(queries)
    heads_here = width // HEAD_DIM
    group = heads_here * quarters // (key_vectors.shape[1] // HEAD_DIM)
    kv_head = lax.axis_index("cp") * heads_here // group
    keys = lax.dynamic_slice_in_dim(key_vectors, kv_head * HEAD_DIM, HEAD_DIM, 1)
    values = lax.dynamic_slice_in_dim(value_vectors, kv_head * HEAD_DIM, HEAD_DIM, 1)
    probs = attention_probs(my_queries, keys, seen_keys(block_mask[0], tokens))
    early = lax.optimization_barrier((outgoing[1], w_down[0].T, in_part))
    outgoing[1], down_t, in_part = early

    def exchange(rows):
        rows = swap(rows.reshape(experts, 2 * share, half), "ep")
        return rows.reshape(2 * part_rows, half)

    arrived = exchange(outgoing[0])
    first_sum, rows = lax.optimization_barrier((project_down(arrived, down_t), outgoing[1]))
    hidden_grad = lax.psum(first_sum, "cp")
    arrived = exchange(rows)
    saved = turn_saved(saved, share)
    rows = expert_rows(hidden_grad, saved[0], saved[1], w_gate[0], w_up[0])
    arrived, rows, saved = lax.optimization_barrier((arrived, rows, saved))
    later_sum = project_down(arrived, down_t)
    rows, _ = lax.optimization_barrier((rows, later_sum))
    back = [list(range(quarters))[::-1]]
    later_grad = lax.psum(later_sum, "cp", axis_index_groups=back)
    returned = exchange(rows)
    returned_later = exchange(expert_rows(later_grad, saved[2], saved[3], w_gate[0], w_up[0]))

    total = collect_rows(in_part[0], returned, grad_out, f32)
    ready = (returned_later, total, probs, my_queries, values, keys.T)
    returned_later, total, probs, my_queries, values, keys_t = lax.optimization_barrier(ready)
    local_grad = collect_rows(in_part[1], returned_later, total, bf16)
    grad_hidden = to_rows(local_grad)
    packed = attention_grads(probs, local_grad, my_queries, values, keys_t)
    packed, grad_hidden = lax.optimization_barrier((packed, grad_hidden))
    packed = swap(packed.reshape(quarters, tokens // quarters, -1), "cp")
    grad_query = packed[:, :, :width].transpose(1, 0, 2).reshape(tokens // quarters, -1)
    sums = packed[:, :, width:].astype(f32)
    sums = sums.reshape(quarters * heads_here // group, -1, tokens // quarters, 2, HEAD_DIM)
    sums = jnp.sum(sums, axis=1).transpose(2, 1, 0, 3).reshape(2, tokens // quarters, -1)
    sums = sums.astype(bf16)
    return (grad_hidden, grad_query, sums[0], sums[1])


def solution(mesh):
    in_specs = (
        P("ep", "cp"),
        P("ep", None),
        P("ep", None),
        P("ep", None),
        P("ep", None),
        P("ep", None, "cp"),
        P("ep", None, "cp"),
        P("ep", None, "cp"),
        P("ep", "cp", None),
        P("ep", "cp", None),
        P(("ep", "cp"), None),
        P("ep", None),
        P("ep", None),
        P("ep", None, None),
    )
    out_specs = (
        P(("ep", "cp"), None),
        P(("ep", "cp"), None),
        P(("ep", "cp"), None),
        P(("ep", "cp"), None),
    )
    return jax.shard_map(
        on_device, mesh=mesh, in_specs=in_specs, out_specs=out_specs, check_vma=False
    )
```

```python
import functools

import jax
import jax.numpy as jnp
from jax import lax
from jax.experimental import pallas as pl
from jax.experimental.pallas import tpu as pltpu
from jax.sharding import PartitionSpec as P

HEAD_DIM = 128
LANES = 128
PARTS = 2
STEPS = 4
CHOSEN_STEPS = 2
DOWN_STEPS = 3
LAST_SHARE = 4
VMEM_LIMIT = 56 * 1024 * 1024
SMALL_VMEM = 24 * 1024 * 1024

f32 = jnp.float32
bf16 = jnp.bfloat16


def params(limit=VMEM_LIMIT):
    return pltpu.CompilerParams(vmem_limit_bytes=limit)


def stay(*arrays):
    return [pltpu.with_memory_space_constraint(a, pltpu.HBM) for a in arrays]


def cost(flops, moved, exps=0):
    return pl.CostEstimate(flops=flops, bytes_accessed=moved, transcendentals=exps)


def weave(out_ref, wide, low, high):
    rows = low.shape[0]
    for j in range(wide.shape[0]):
        cols = slice(j * LANES, (j + 1) * LANES)
        wide[j, pl.ds(0, rows, 2), :] = low[:, cols]
        wide[j, pl.ds(1, rows, 2), :] = high[:, cols]
        out_ref[:, cols] = wide[j].astype(bf16)


def unweave(rows_ref, wide):
    slabs, rows = wide.shape[0], wide.shape[1] // 2
    for j in range(slabs):
        wide[j] = rows_ref[:, j * LANES : (j + 1) * LANES].astype(f32)
    low = [wide[j, pl.ds(0, rows, 2), :].astype(bf16) for j in range(slabs)]
    high = [wide[j, pl.ds(1, rows, 2), :].astype(bf16) for j in range(slabs)]
    return jnp.concatenate(low, axis=1), jnp.concatenate(high, axis=1)


def woven(rows, half):
    return pltpu.VMEM((half // LANES, 2 * rows, LANES), f32)


def split_by(row, size, count):
    factor = (1 << 16) // size + 1
    assert all((r * factor) >> 16 == r // size for r in range(count))
    return (row * factor) >> 16


def route_rows(part, capacity, ids_ref, spare_ref, slot_ref, probs_ref, grad_ref, out_ref, wide):
    rows, half = out_ref.shape[0] // 2, out_ref.shape[1]
    tokens = grad_ref.shape[0]
    share = capacity // PARTS
    overflow = slot_ref[...] >= capacity
    expert = jnp.where(overflow, spare_ref[...], ids_ref[...])
    target = expert * capacity + slot_ref[...] - jnp.where(overflow, capacity, 0)
    row = lax.broadcasted_iota(jnp.int32, (rows, 1), 0) + pl.program_id(0) * rows
    group = split_by(row, share, rows * STEPS)
    dest = group * (capacity - share) + row + part * share
    weights = jnp.zeros((rows, tokens), f32)
    for k in range(target.shape[0]):
        weights = jnp.where(target[k : k + 1, :] == dest, probs_ref[k : k + 1, :], weights)
    weight = jnp.sum(weights, axis=1, keepdims=True)
    chosen = jnp.where(weights != 0.0, 1.0, 0.0).astype(bf16)
    picked = jnp.dot(chosen, grad_ref[...], preferred_element_type=f32)
    picked = picked * weight
    weave(out_ref, wide, picked[:, :half], picked[:, half:])


def send_rows(part, experts, capacity, ids, spare, slots, probs, grad):
    rows, (tokens, width) = experts * capacity // PARTS, grad.shape
    step, half = rows // STEPS, width // 2
    routes = pl.BlockSpec(slots.shape, lambda i: (0, 0))
    return pl.pallas_call(
        functools.partial(route_rows, part, capacity),
        grid=(STEPS,),
        in_specs=[routes] * 4 + [pl.BlockSpec(grad.shape, lambda i: (0, 0))],
        out_specs=pl.BlockSpec((2 * step, half), lambda i: (i, 0)),
        out_shape=pltpu.HBM((2 * rows, half), bf16),
        scratch_shapes=[woven(step, half)],
        compiler_params=params(),
        cost_estimate=cost(2 * rows * tokens * width, 4 * rows * width),
        name="send_rows",
    )(ids, spare, slots, probs, *stay(grad))


def turn_kernel(share, saved_ref, *refs):
    outs, tall = refs[:-1], refs[-1]
    quarters, kinds = saved_ref.shape[:2]
    groups = saved_ref.shape[3] // (PARTS * share)
    for kind in range(kinds):
        hidden = jnp.concatenate([saved_ref[c, kind] for c in range(quarters)], axis=0)
        rows = hidden.astype(f32).T
        for part in range(PARTS):
            for g in range(groups):
                start = (g * PARTS + part) * share
                tall[g * share : (g + 1) * share, :] = rows[start : start + share, :]
            outs[part * kinds + kind][...] = tall[...].astype(bf16)


def turn_saved(saved, share):
    quarters, kinds, units, slots = saved.shape
    hidden, rows = quarters * units, slots // PARTS
    step = rows // STEPS
    return pl.pallas_call(
        functools.partial(turn_kernel, share),
        grid=(STEPS,),
        in_specs=[pl.BlockSpec((quarters, kinds, units, PARTS * step), lambda i: (0, 0, 0, i))],
        out_specs=[pl.BlockSpec((step, hidden), lambda i: (i, 0))] * (PARTS * kinds),
        out_shape=[jax.ShapeDtypeStruct((rows, hidden), bf16)] * (PARTS * kinds),
        scratch_shapes=[pltpu.VMEM((step, hidden), f32)],
        compiler_params=params(),
        cost_estimate=cost(saved.size, 4 * saved.size),
        name="turn_saved",
    )(saved)


def turn_kernel_2d(in_ref, out_ref):
    out_ref[...] = in_ref[...].astype(f32).T.astype(bf16)


def turn_weights(weights):
    hidden, width = weights.shape
    step = hidden // DOWN_STEPS
    return pl.pallas_call(
        turn_kernel_2d,
        grid=(DOWN_STEPS,),
        in_specs=[pl.BlockSpec((step, width), lambda i: (i, 0))],
        out_specs=pl.BlockSpec((width, step), lambda i: (0, i)),
        out_shape=pltpu.HBM((width, hidden), bf16),
        compiler_params=params(SMALL_VMEM),
        cost_estimate=cost(weights.size, 4 * weights.size),
        name="turn_weights",
    )(*stay(weights))


def down_rows_kernel(rows_ref, down_ref, out_ref, wide):
    half = rows_ref.shape[1]
    low, high = unweave(rows_ref, wide)
    total = jnp.dot(low, down_ref[:half, :], preferred_element_type=f32)
    total = total + jnp.dot(high, down_ref[half:, :], preferred_element_type=f32)
    out_ref[...] = total.astype(bf16)


def project_down(arrived, down_t):
    rows, half = arrived.shape[0] // 2, arrived.shape[1]
    width, hidden = down_t.shape
    step = rows // STEPS
    return pl.pallas_call(
        down_rows_kernel,
        grid=(STEPS,),
        in_specs=[
            pl.BlockSpec((2 * step, half), lambda i: (i, 0)),
            pl.BlockSpec(down_t.shape, lambda i: (0, 0)),
        ],
        out_specs=pl.BlockSpec((step, hidden), lambda i: (i, 0)),
        out_shape=pltpu.HBM((rows, hidden), bf16),
        scratch_shapes=[woven(step, half)],
        compiler_params=params(SMALL_VMEM),
        cost_estimate=cost(2 * rows * width * hidden, 2 * rows * (width + hidden)),
        name="project_down",
    )(arrived, *stay(down_t))


def expert_kernel(hidden_ref, gate_ref, up_ref, wg_ref, wu_ref, *refs):
    outs, wides = refs[: len(refs) // 2], refs[len(refs) // 2 :]
    grad = hidden_ref[...].astype(f32)
    gate = gate_ref[...].astype(f32)
    up = up_ref[...].astype(f32)
    sig = 1.0 / (1.0 + jnp.exp(-gate))
    shared = grad * sig
    gate_grad = (shared * up * (1.0 + gate * (1.0 - sig))).astype(bf16)
    up_grad = (shared * gate).astype(bf16)
    total = jnp.dot(gate_grad, wg_ref[...], preferred_element_type=f32)
    total = total + jnp.dot(up_grad, wu_ref[...], preferred_element_type=f32)
    start = 0
    for out_ref, wide in zip(outs, wides):
        half = out_ref.shape[1]
        low, high = total[:, start : start + half], total[:, start + half : start + 2 * half]
        weave(out_ref, wide, low, high)
        start += 2 * half


def expert_rows(hidden_grad, gate, up, w_gate, w_up, widths):
    rows, hidden = hidden_grad.shape
    step, width = rows // STEPS, sum(widths)
    row_block = pl.BlockSpec((step, hidden), lambda i: (i, 0))
    whole = pl.BlockSpec(w_gate.shape, lambda i: (0, 0))
    return pl.pallas_call(
        expert_kernel,
        grid=(STEPS,),
        in_specs=[row_block, row_block, row_block, whole, whole],
        out_specs=[pl.BlockSpec((2 * step, w // 2), lambda i: (i, 0)) for w in widths],
        out_shape=[jax.ShapeDtypeStruct((2 * rows, w // 2), bf16) for w in widths],
        scratch_shapes=[woven(step, w // 2) for w in widths],
        compiler_params=params(),
        cost_estimate=cost(
            128 * rows * hidden * width, 2 * rows * (3 * hidden + width), rows * hidden
        ),
        name="expert_rows",
    )(hidden_grad, gate, up, w_gate, w_up)


def chosen_kernel(slots_ref, out_ref):
    tokens, rows = out_ref.shape
    row = lax.broadcasted_iota(jnp.int32, (tokens, rows), 1) + pl.program_id(0) * rows
    chosen = jnp.zeros((tokens, rows), f32)
    for k in range(slots_ref.shape[1]):
        chosen = jnp.where(slots_ref[:, k : k + 1] == row, 1.0, chosen)
    out_ref[...] = chosen.astype(bf16)


def chosen_rows(slots, rows):
    tokens = slots.shape[0]
    step = rows // CHOSEN_STEPS
    return pl.pallas_call(
        chosen_kernel,
        grid=(CHOSEN_STEPS,),
        in_specs=[pl.BlockSpec(slots.shape, lambda i: (0, 0))],
        out_specs=pl.BlockSpec((tokens, step), lambda i: (0, i)),
        out_shape=pltpu.HBM((tokens, rows), bf16),
        compiler_params=params(SMALL_VMEM),
        cost_estimate=cost(8 * tokens * rows, 2 * tokens * rows),
        name="chosen_rows",
    )(slots)


def collect_kernel(chosen_ref, rows_ref, base_ref, out_ref, total, wide):
    step = pl.program_id(0)
    half = rows_ref.shape[1]

    @pl.when(step == 0)
    def _():
        total[...] = base_ref[...].astype(f32)

    low, high = unweave(rows_ref, wide)
    total[:, :half] += jnp.dot(chosen_ref[...], low, preferred_element_type=f32)
    total[:, half:] += jnp.dot(chosen_ref[...], high, preferred_element_type=f32)

    @pl.when(step == CHOSEN_STEPS - 1)
    def _():
        out_ref[...] = total[...].astype(out_ref.dtype)


def collect_rows(chosen, returned, base, start, out_dtype):
    rows, half = returned.shape[0] // 2, returned.shape[1]
    tokens, width = base.shape[0], 2 * half
    step, column = rows // CHOSEN_STEPS, start // width
    assert column * width == start
    return pl.pallas_call(
        collect_kernel,
        grid=(CHOSEN_STEPS,),
        in_specs=[
            pl.BlockSpec((tokens, step), lambda i: (0, i)),
            pl.BlockSpec((2 * step, half), lambda i: (i, 0)),
            pl.BlockSpec((tokens, width), lambda i: (0, column)),
        ],
        out_specs=pl.BlockSpec((tokens, width), lambda i: (0, 0)),
        out_shape=jax.ShapeDtypeStruct((tokens, width), out_dtype),
        scratch_shapes=[pltpu.VMEM((tokens, width), f32), woven(step, half)],
        compiler_params=params(SMALL_VMEM),
        cost_estimate=cost(2 * rows * tokens * width, 2 * rows * width + 8 * tokens * width),
        name="collect_rows",
    )(*stay(chosen), returned, *stay(base))


def probs_kernel(q_ref, k_ref, seen_ref, out_ref):
    length = q_ref.shape[0]
    block = length // 2
    scale = HEAD_DIM ** (-0.5)
    for part in range(2):
        keys = (part + 1) * block
        cols = slice(part * block, (part + 1) * block)
        scores = lax.dot_general(
            k_ref[:keys, :], q_ref[cols, :], (((1,), (1,)), ((), ())), preferred_element_type=f32
        )
        scores = jnp.where(seen_ref[:keys, cols] > 0, scores * scale, -jnp.inf)
        peak = jnp.max(scores, axis=0, keepdims=True)
        exponent = jnp.exp(scores - peak)
        out_ref[0, :keys, cols] = exponent / jnp.sum(exponent, axis=0, keepdims=True)
        if keys < length:
            out_ref[0, keys:, cols] = jnp.zeros((length - keys, block), f32)


def attention_probs(queries, keys, seen):
    length, heads = queries.shape[0], queries.shape[1] // HEAD_DIM
    return pl.pallas_call(
        probs_kernel,
        grid=(heads,),
        in_specs=[
            pl.BlockSpec((length, HEAD_DIM), lambda h: (0, h)),
            pl.BlockSpec(keys.shape, lambda h: (0, 0)),
            pl.BlockSpec(seen.shape, lambda h: (0, 0)),
        ],
        out_specs=pl.BlockSpec((1, length, length), lambda h: (h, 0, 0)),
        out_shape=pltpu.HBM((heads, length, length), f32),
        compiler_params=params(SMALL_VMEM),
        cost_estimate=cost(
            2 * heads * length * length * HEAD_DIM,
            4 * heads * length * length,
            heads * length * length,
        ),
        name="attention_probs",
    )(queries, keys, seen)


def head_grads(probs_ref, grad_ref, q_ref, v_ref, kt_ref, out_ref, sum_k, sum_v):
    length = q_ref.shape[0]
    block = length // 2
    scale = HEAD_DIM ** (-0.5)
    for part in range(2):
        keys = (part + 1) * block
        cols = slice(part * block, (part + 1) * block)
        probs = probs_ref[0, :keys, cols]
        grad = grad_ref[cols, :]
        prob_grad = lax.dot_general(
            v_ref[:keys, :], grad, (((1,), (1,)), ((), ())), preferred_element_type=f32
        )
        row_total = jnp.sum(probs * prob_grad, axis=0, keepdims=True)
        score_grad = (probs * (prob_grad - row_total)).astype(bf16)
        query_grad = jnp.dot(kt_ref[:, :keys], score_grad, preferred_element_type=f32) * scale
        out_ref[cols, :] = query_grad.T.astype(bf16)
        sum_k[:keys, :] += jnp.dot(score_grad, q_ref[cols, :], preferred_element_type=f32)
        sum_v[:keys, :] += jnp.dot(probs.astype(bf16), grad, preferred_element_type=f32)


def first_grads_kernel(probs_ref, grad_ref, q_ref, v_ref, kt_ref, out_ref, sum_k, sum_v):
    @pl.when(pl.program_id(0) == 0)
    def _():
        sum_k[...] = jnp.zeros_like(sum_k)
        sum_v[...] = jnp.zeros_like(sum_v)

    head_grads(probs_ref, grad_ref, q_ref, v_ref, kt_ref, out_ref, sum_k, sum_v)


def last_grads_kernel(
    probs_ref, grad_ref, q_ref, v_ref, kt_ref, old_k, old_v, out_ref, sum_k, sum_v
):
    head, heads = pl.program_id(0), pl.num_programs(0)
    scale = HEAD_DIM ** (-0.5)

    @pl.when(head == 0)
    def _():
        sum_k[...] = old_k[...]
        sum_v[...] = old_v[...]

    first = pl.multiple_of((head + 2) * HEAD_DIM, HEAD_DIM)
    out_ref[:, pl.ds(first, HEAD_DIM)] = grad_ref[...]
    first = pl.multiple_of((head + heads + 2) * HEAD_DIM, HEAD_DIM)
    out = out_ref.at[:, pl.ds(first, HEAD_DIM)]
    head_grads(probs_ref, grad_ref, q_ref, v_ref, kt_ref, out, sum_k, sum_v)

    @pl.when(head == heads - 1)
    def _():
        out_ref[:, :HEAD_DIM] = (sum_k[...] * scale).astype(bf16)
        out_ref[:, HEAD_DIM : 2 * HEAD_DIM] = sum_v[...].astype(bf16)


def attention_grads(probs, out_grad, queries, values, keys_t, first, sums=None):
    length, heads = out_grad.shape[0], out_grad.shape[1] // HEAD_DIM
    whole = pl.BlockSpec((length, HEAD_DIM), lambda h: (0, 0))
    totals = [jax.ShapeDtypeStruct((length, HEAD_DIM), f32)] * 2
    out_spec = pl.BlockSpec((length, HEAD_DIM), lambda h: (0, h))
    in_specs = [
        pl.BlockSpec((1, length, length), lambda h: (first + h, 0, 0)),
        out_spec,
        pl.BlockSpec((length, HEAD_DIM), lambda h: (0, first + h)),
        whole,
        pl.BlockSpec(keys_t.shape, lambda h: (0, 0)),
    ]
    estimate = cost(8 * heads * length * length * HEAD_DIM, 4 * heads * length * length)
    operands = (*stay(probs), out_grad, *stay(queries), values, keys_t)
    if sums is None:
        return pl.pallas_call(
            first_grads_kernel,
            grid=(heads,),
            in_specs=in_specs,
            out_specs=[out_spec, whole, whole],
            out_shape=[jax.ShapeDtypeStruct(out_grad.shape, bf16)] + totals,
            compiler_params=params(SMALL_VMEM),
            cost_estimate=estimate,
            name="first_grads",
        )(*operands)
    columns = (2 * heads + 2) * HEAD_DIM
    return pl.pallas_call(
        last_grads_kernel,
        grid=(heads,),
        in_specs=in_specs + [whole, whole],
        out_specs=pl.BlockSpec((length, columns), lambda h: (0, 0)),
        out_shape=jax.ShapeDtypeStruct((length, columns), bf16),
        scratch_shapes=[pltpu.VMEM((length, HEAD_DIM), f32)] * 2,
        compiler_params=params(SMALL_VMEM),
        cost_estimate=estimate,
        name="last_grads",
    )(*operands, *sums)


def pass_round(pieces):
    parts = lax.axis_size("cp")
    me = lax.axis_index("cp")
    got = []
    for shift in range(parts):
        piece = pieces((me + shift) % parts)
        if shift:
            piece = lax.ppermute(piece, "cp", [(i, (i + shift) % parts) for i in range(parts)])
        got.append((piece, (me - shift) % parts))
    return got


def to_heads(queries):
    parts = lax.axis_size("cp")
    rows, width = queries.shape[0], queries.shape[1] // parts
    out = jnp.zeros((parts * rows, width), queries.dtype)
    for piece, i in pass_round(lambda i: lax.dynamic_slice_in_dim(queries, i * width, width, 1)):
        out = lax.dynamic_update_slice(out, piece, (i * rows, 0))
    return out


def to_rows(grads):
    rows = grads.shape[0] // lax.axis_size("cp")
    return pass_round(lambda i: lax.dynamic_slice_in_dim(grads, i * rows, rows, 0))


def join_rows(pieces, most, width):
    rows = pieces[0][0].shape[0]
    out = jnp.zeros((rows, len(pieces) * width), bf16)
    for piece, i in pieces:
        out = lax.dynamic_update_slice(out, piece, (0, i * width))
    return out


def finish_kernel(last, together, got_ref, *refs):
    grad_ref, query_ref, key_ref, value_ref, sum_k, sum_v = refs[2:]
    place = pl.program_id(0) % together
    key = got_ref[0, :, :HEAD_DIM].astype(f32)
    value = got_ref[0, :, HEAD_DIM : 2 * HEAD_DIM].astype(f32)
    grad_ref[...] = got_ref[0, :, 2 * HEAD_DIM : 2 * HEAD_DIM + last]
    query_ref[...] = got_ref[0, :, 2 * HEAD_DIM + last :]

    @pl.when(place == 0)
    def _():
        sum_k[...] = key
        sum_v[...] = value

    @pl.when(place > 0)
    def _():
        sum_k[...] += key
        sum_v[...] += value

    key_ref[...] = sum_k[...].astype(bf16)
    value_ref[...] = sum_v[...].astype(bf16)


def finish(got, grad_hidden, grad_query, together):
    parts, rows, columns = got.shape
    last = (columns - 2 * HEAD_DIM) // 2
    ratio = grad_hidden.shape[1] // parts // last
    rest = pl.BlockSpec((rows, last), lambda i: (0, i * ratio + ratio - 1))
    sums = pl.BlockSpec((rows, HEAD_DIM), lambda i: (0, i // together))
    sums_shape = jax.ShapeDtypeStruct((rows, parts // together * HEAD_DIM), bf16)
    return pl.pallas_call(
        functools.partial(finish_kernel, last, together),
        grid=(parts,),
        in_specs=[
            pl.BlockSpec((1, rows, columns), lambda i: (i, 0, 0)),
            pl.BlockSpec(memory_space=pl.ANY),
            pl.BlockSpec(memory_space=pl.ANY),
        ],
        out_specs=[rest, rest, sums, sums],
        out_shape=[
            jax.ShapeDtypeStruct(grad_hidden.shape, bf16),
            jax.ShapeDtypeStruct(grad_query.shape, bf16),
            sums_shape,
            sums_shape,
        ],
        input_output_aliases={1: 0, 2: 1},
        scratch_shapes=[pltpu.VMEM((rows, HEAD_DIM), f32)] * 2,
        compiler_params=params(SMALL_VMEM),
        cost_estimate=cost(4 * got.size, 4 * got.size),
        name="finish",
    )(got, grad_hidden, grad_query)


def seen_keys(mask_table, length):
    blocks = mask_table.shape[0]
    size = length // blocks
    pos = jnp.arange(length, dtype=jnp.int32)
    near = jnp.broadcast_to(mask_table.T[:, None, :, None], (blocks, size, blocks, size))
    near = near.reshape(length, length) > 0
    same = (pos // size)[:, None] == (pos // size)[None, :]
    return ((pos[:, None] <= pos[None, :]) & (same | near)).astype(f32)


def swap(rows, axis):
    return lax.all_to_all(rows, axis, split_axis=0, concat_axis=0, tiled=True)


def on_device(
    grad_out,
    route_ids,
    fallback_ids,
    slot_ids,
    route_probs,
    w_gate,
    w_up,
    w_down,
    gate_pre,
    up_pre,
    queries,
    key_vectors,
    value_vectors,
    block_mask,
):
    experts = lax.axis_size("ep")
    quarters = lax.axis_size("cp")
    tokens, width = grad_out.shape
    slot_count = gate_pre.shape[2]
    capacity = slot_count // experts
    share = capacity // PARTS
    part_rows = experts * share
    half = width // 2

    routes = (route_ids.T, fallback_ids.T, slot_ids.T)
    probs_t = route_probs.T
    outgoing = [
        send_rows(part, experts, capacity, *routes, probs_t, grad_out) for part in range(PARTS)
    ]
    saved = lax.all_gather(jnp.stack([gate_pre[0], up_pre[0]]), "cp", axis=0)

    overflow = routes[2] >= capacity
    expert = jnp.where(overflow, routes[1], routes[0])
    slot = routes[2] - jnp.where(overflow, capacity, 0)
    in_part = [
        jnp.where(slot // share == part, expert * share + slot - part * share, -1).T
        for part in range(PARTS)
    ]
    my_queries = to_heads(queries)
    heads_here = width // HEAD_DIM
    group = heads_here * quarters // (key_vectors.shape[1] // HEAD_DIM)
    kv_head = lax.axis_index("cp") * heads_here // group
    keys = lax.dynamic_slice_in_dim(key_vectors, kv_head * HEAD_DIM, HEAD_DIM, 1)
    values = lax.dynamic_slice_in_dim(value_vectors, kv_head * HEAD_DIM, HEAD_DIM, 1)
    probs = attention_probs(my_queries, keys, seen_keys(block_mask[0], tokens))
    early = lax.optimization_barrier((outgoing[1], turn_weights(w_down[0]), in_part))
    outgoing[1], down_t, in_part = early

    def exchange(rows):
        wide = rows.shape[1]
        rows = swap(rows.reshape(experts, 2 * share, wide), "ep")
        return rows.reshape(2 * part_rows, wide)

    arrived = exchange(outgoing[0])
    first_sum, rows = lax.optimization_barrier((project_down(arrived, down_t), outgoing[1]))
    hidden_grad = lax.psum(first_sum, "cp")
    arrived = exchange(rows)
    saved = turn_saved(saved, share)
    (rows,) = expert_rows(hidden_grad, saved[0], saved[1], w_gate[0], w_up[0], [width])
    arrived, rows, saved = lax.optimization_barrier((arrived, rows, saved))
    later_sum = project_down(arrived, down_t)
    rows, _ = lax.optimization_barrier((rows, later_sum))
    back = [list(range(quarters))[::-1]]
    later_grad = lax.psum(later_sum, "cp", axis_index_groups=back)
    returned = exchange(rows)
    last = width // LAST_SHARE
    most = width - last
    rows = expert_rows(later_grad, saved[2], saved[3], w_gate[0], w_up[0], [most, last])
    returned_most = exchange(rows[0])
    chosen = [chosen_rows(slots, part_rows) for slots in in_part]
    total = collect_rows(chosen[0], *stay(returned), grad_out, 0, f32)
    ready = (returned_most, rows[1], chosen, total, probs, my_queries, values, keys.T)
    ready = lax.optimization_barrier(ready)
    returned_most, last_rows, chosen, total, probs, my_queries, values, keys_t = ready
    returned_last = exchange(last_rows)

    most_grad = collect_rows(chosen[1], returned_most, total, 0, bf16)
    grad_pieces = to_rows(most_grad)
    query_part, *sums = attention_grads(probs, most_grad, my_queries, values, keys_t, 0)
    query_pieces = to_rows(query_part)

    last_grad = collect_rows(chosen[1], returned_last, total, most, bf16)
    packed = attention_grads(
        probs, last_grad, my_queries, values, keys_t, most // HEAD_DIM, sums
    )
    ready = (packed, [p for p, _ in grad_pieces], [p for p, _ in query_pieces])
    packed, grads, query_grads = lax.optimization_barrier(ready)
    rows_here = tokens // quarters
    packed = swap(packed.reshape(quarters, rows_here, -1), "cp")
    grad_hidden = join_rows([(p, i) for p, (_, i) in zip(grads, grad_pieces)], most, width)
    grad_query = join_rows([(p, i) for p, (_, i) in zip(query_grads, query_pieces)], most, width)
    return finish(packed, grad_hidden, grad_query, group // heads_here)


def solution(mesh):
    in_specs = (
        P("ep", "cp"),
        P("ep", None),
        P("ep", None),
        P("ep", None),
        P("ep", None),
        P("ep", None, "cp"),
        P("ep", None, "cp"),
        P("ep", None, "cp"),
        P("ep", "cp", None),
        P("ep", "cp", None),
        P(("ep", "cp"), None),
        P("ep", None),
        P("ep", None),
        P("ep", None, None),
    )
    out_specs = (
        P(("ep", "cp"), None),
        P(("ep", "cp"), None),
        P(("ep", "cp"), None),
        P(("ep", "cp"), None),
    )
    return jax.shard_map(
        on_device, mesh=mesh, in_specs=in_specs, out_specs=out_specs, check_vma=False
    )
```

```python
import functools

import jax
import jax.numpy as jnp
from jax import lax
from jax.experimental import pallas as pl
from jax.experimental.pallas import tpu as pltpu
from jax.sharding import PartitionSpec as P

HEAD_DIM = 128
LANES = 128
PARTS = 2
STEPS = 4
CHOSEN_STEPS = 2
DOWN_STEPS = 3
DOWN_COLS = 256
PROJECT_STEPS = 2
LAST_SHARE = 4
VMEM_LIMIT = 56 * 1024 * 1024
SMALL_VMEM = 24 * 1024 * 1024

f32 = jnp.float32
bf16 = jnp.bfloat16


def params(limit=VMEM_LIMIT):
    return pltpu.CompilerParams(vmem_limit_bytes=limit)


def stay(*arrays):
    return [pltpu.with_memory_space_constraint(a, pltpu.HBM) for a in arrays]


def cost(flops, moved, exps=0):
    return pl.CostEstimate(flops=flops, bytes_accessed=moved, transcendentals=exps)


def weave(out_ref, wide, low, high):
    rows = low.shape[0]
    for j in range(wide.shape[0]):
        cols = slice(j * LANES, (j + 1) * LANES)
        wide[j, pl.ds(0, rows, 2), :] = low[:, cols]
        wide[j, pl.ds(1, rows, 2), :] = high[:, cols]
        out_ref[:, cols] = wide[j, : 2 * rows, :].astype(bf16)


def unweave(rows_ref, wide):
    slabs, rows = wide.shape[0], rows_ref.shape[0] // 2
    for j in range(slabs):
        wide[j, : 2 * rows, :] = rows_ref[:, j * LANES : (j + 1) * LANES].astype(f32)
    low = [wide[j, pl.ds(0, rows, 2), :].astype(bf16) for j in range(slabs)]
    high = [wide[j, pl.ds(1, rows, 2), :].astype(bf16) for j in range(slabs)]
    return jnp.concatenate(low, axis=1), jnp.concatenate(high, axis=1)


def woven(rows, half):
    return pltpu.VMEM((half // LANES, 2 * rows + 8, LANES), f32)


def split_by(row, size, count):
    factor = (1 << 16) // size + 1
    assert all((r * factor) >> 16 == r // size for r in range(count))
    return (row * factor) >> 16


def route_rows(part, capacity, ids_ref, spare_ref, slot_ref, probs_ref, grad_ref, out_ref, wide):
    rows, half = out_ref.shape[0] // 2, out_ref.shape[1]
    tokens = grad_ref.shape[0]
    share = capacity // PARTS
    overflow = slot_ref[...] >= capacity
    expert = jnp.where(overflow, spare_ref[...], ids_ref[...])
    target = expert * capacity + slot_ref[...] - jnp.where(overflow, capacity, 0)
    row = lax.broadcasted_iota(jnp.int32, (rows, 1), 0) + pl.program_id(0) * rows
    group = split_by(row, share, rows * STEPS)
    dest = group * (capacity - share) + row + part * share
    weights = jnp.zeros((rows, tokens), f32)
    for k in range(target.shape[0]):
        weights = jnp.where(target[k : k + 1, :] == dest, probs_ref[k : k + 1, :], weights)
    weight = jnp.sum(weights, axis=1, keepdims=True)
    chosen = jnp.where(weights != 0.0, 1.0, 0.0).astype(bf16)
    picked = jnp.dot(chosen, grad_ref[...], preferred_element_type=f32)
    picked = picked * weight
    weave(out_ref, wide, picked[:, :half], picked[:, half:])


def send_rows(part, experts, capacity, ids, spare, slots, probs, grad):
    rows, (tokens, width) = experts * capacity // PARTS, grad.shape
    step, half = rows // STEPS, width // 2
    routes = pl.BlockSpec(slots.shape, lambda i: (0, 0))
    return pl.pallas_call(
        functools.partial(route_rows, part, capacity),
        grid=(STEPS,),
        in_specs=[routes] * 4 + [pl.BlockSpec(grad.shape, lambda i: (0, 0))],
        out_specs=pl.BlockSpec((2 * step, half), lambda i: (i, 0)),
        out_shape=pltpu.HBM((2 * rows, half), bf16),
        scratch_shapes=[woven(step, half)],
        compiler_params=params(),
        cost_estimate=cost(2 * rows * tokens * width, 4 * rows * width),
        name="send_rows",
    )(ids, spare, slots, probs, *stay(grad))


def turn_kernel(share, saved_ref, *refs):
    outs, tall = refs[:-1], refs[-1]
    quarters, kinds = saved_ref.shape[:2]
    groups = saved_ref.shape[3] // (PARTS * share)
    for kind in range(kinds):
        hidden = jnp.concatenate([saved_ref[c, kind] for c in range(quarters)], axis=0)
        rows = hidden.astype(f32).T
        for part in range(PARTS):
            for g in range(groups):
                start = (g * PARTS + part) * share
                tall[g * share : (g + 1) * share, :] = rows[start : start + share, :]
            outs[part * kinds + kind][...] = tall[...].astype(bf16)


def turn_saved(saved, share):
    quarters, kinds, units, slots = saved.shape
    hidden, rows = quarters * units, slots // PARTS
    step = rows // STEPS
    return pl.pallas_call(
        functools.partial(turn_kernel, share),
        grid=(STEPS,),
        in_specs=[pl.BlockSpec((quarters, kinds, units, PARTS * step), lambda i: (0, 0, 0, i))],
        out_specs=[pl.BlockSpec((step, hidden), lambda i: (i, 0))] * (PARTS * kinds),
        out_shape=[jax.ShapeDtypeStruct((rows, hidden), bf16)] * (PARTS * kinds),
        scratch_shapes=[pltpu.VMEM((step, hidden), f32)],
        compiler_params=params(),
        cost_estimate=cost(saved.size, 4 * saved.size),
        name="turn_saved",
    )(saved)


def turn_kernel_2d(in_ref, out_ref):
    out_ref[...] = in_ref[...].astype(f32).T.astype(bf16)


def turn_weights(weights):
    hidden, width = weights.shape
    step = hidden // DOWN_STEPS
    return pl.pallas_call(
        turn_kernel_2d,
        grid=(DOWN_STEPS,),
        in_specs=[pl.BlockSpec((step, width), lambda i: (i, 0))],
        out_specs=pl.BlockSpec((width, step), lambda i: (0, i)),
        out_shape=pltpu.HBM((width, hidden), bf16),
        compiler_params=params(SMALL_VMEM),
        cost_estimate=cost(weights.size, 4 * weights.size),
        name="turn_weights",
    )(*stay(weights))


def down_rows_kernel(rows_ref, down_ref, out_ref, wide):
    half = rows_ref.shape[1]
    low, high = unweave(rows_ref, wide)
    for start in range(0, down_ref.shape[1], DOWN_COLS):
        cols = slice(start, start + DOWN_COLS)
        total = jnp.dot(low, down_ref[:half, cols], preferred_element_type=f32)
        total = total + jnp.dot(high, down_ref[half:, cols], preferred_element_type=f32)
        out_ref[:, cols] = total.astype(bf16)


def project_down(arrived, down_t):
    rows, half = arrived.shape[0] // 2, arrived.shape[1]
    width, hidden = down_t.shape
    step = rows // PROJECT_STEPS
    return pl.pallas_call(
        down_rows_kernel,
        grid=(PROJECT_STEPS,),
        in_specs=[
            pl.BlockSpec((2 * step, half), lambda i: (i, 0)),
            pl.BlockSpec(down_t.shape, lambda i: (0, 0)),
        ],
        out_specs=pl.BlockSpec((step, hidden), lambda i: (i, 0)),
        out_shape=pltpu.HBM((rows, hidden), bf16),
        scratch_shapes=[woven(step, half)],
        compiler_params=params(SMALL_VMEM),
        cost_estimate=cost(2 * rows * width * hidden, 2 * rows * (width + hidden)),
        name="project_down",
    )(arrived, *stay(down_t))


def expert_kernel(hidden_ref, gate_ref, up_ref, wg_ref, wu_ref, *refs):
    outs, wides = refs[: len(refs) // 2], refs[len(refs) // 2 :]
    grad = hidden_ref[...].astype(f32)
    gate = gate_ref[...].astype(f32)
    up = up_ref[...].astype(f32)
    sig = 1.0 / (1.0 + jnp.exp(-gate))
    shared = grad * sig
    gate_grad = (shared * up * (1.0 + gate * (1.0 - sig))).astype(bf16)
    up_grad = (shared * gate).astype(bf16)
    total = jnp.dot(gate_grad, wg_ref[...], preferred_element_type=f32)
    total = total + jnp.dot(up_grad, wu_ref[...], preferred_element_type=f32)
    start = 0
    for out_ref, wide in zip(outs, wides):
        half = out_ref.shape[1]
        low, high = total[:, start : start + half], total[:, start + half : start + 2 * half]
        weave(out_ref, wide, low, high)
        start += 2 * half


def expert_rows(hidden_grad, gate, up, w_gate, w_up, widths):
    rows, hidden = hidden_grad.shape
    step, width = rows // STEPS, sum(widths)
    row_block = pl.BlockSpec((step, hidden), lambda i: (i, 0))
    whole = pl.BlockSpec(w_gate.shape, lambda i: (0, 0))
    return pl.pallas_call(
        expert_kernel,
        grid=(STEPS,),
        in_specs=[row_block, row_block, row_block, whole, whole],
        out_specs=[pl.BlockSpec((2 * step, w // 2), lambda i: (i, 0)) for w in widths],
        out_shape=[jax.ShapeDtypeStruct((2 * rows, w // 2), bf16) for w in widths],
        scratch_shapes=[woven(step, w // 2) for w in widths],
        compiler_params=params(),
        cost_estimate=cost(
            128 * rows * hidden * width, 2 * rows * (3 * hidden + width), rows * hidden
        ),
        name="expert_rows",
    )(hidden_grad, gate, up, w_gate, w_up)


def chosen_kernel(slots_ref, out_ref):
    tokens, rows = out_ref.shape
    row = lax.broadcasted_iota(jnp.int32, (tokens, rows), 1) + pl.program_id(0) * rows
    chosen = jnp.zeros((tokens, rows), f32)
    for k in range(slots_ref.shape[1]):
        chosen = jnp.where(slots_ref[:, k : k + 1] == row, 1.0, chosen)
    out_ref[...] = chosen.astype(bf16)


def chosen_rows(slots, rows):
    tokens = slots.shape[0]
    step = rows // CHOSEN_STEPS
    return pl.pallas_call(
        chosen_kernel,
        grid=(CHOSEN_STEPS,),
        in_specs=[pl.BlockSpec(slots.shape, lambda i: (0, 0))],
        out_specs=pl.BlockSpec((tokens, step), lambda i: (0, i)),
        out_shape=pltpu.HBM((tokens, rows), bf16),
        compiler_params=params(SMALL_VMEM),
        cost_estimate=cost(8 * tokens * rows, 2 * tokens * rows),
        name="chosen_rows",
    )(slots)


def collect_kernel(chosen_ref, rows_ref, base_ref, out_ref, total, wide):
    step = pl.program_id(0)
    half = rows_ref.shape[1]

    @pl.when(step == 0)
    def _():
        total[...] = base_ref[...].astype(f32)

    low, high = unweave(rows_ref, wide)
    total[:, :half] += jnp.dot(chosen_ref[...], low, preferred_element_type=f32)
    total[:, half:] += jnp.dot(chosen_ref[...], high, preferred_element_type=f32)

    @pl.when(step == CHOSEN_STEPS - 1)
    def _():
        out_ref[...] = total[...].astype(out_ref.dtype)


def collect_rows(chosen, returned, base, start, out_dtype):
    rows, half = returned.shape[0] // 2, returned.shape[1]
    tokens, width = base.shape[0], 2 * half
    step, column = rows // CHOSEN_STEPS, start // width
    assert column * width == start
    return pl.pallas_call(
        collect_kernel,
        grid=(CHOSEN_STEPS,),
        in_specs=[
            pl.BlockSpec((tokens, step), lambda i: (0, i)),
            pl.BlockSpec((2 * step, half), lambda i: (i, 0)),
            pl.BlockSpec((tokens, width), lambda i: (0, column)),
        ],
        out_specs=pl.BlockSpec((tokens, width), lambda i: (0, 0)),
        out_shape=jax.ShapeDtypeStruct((tokens, width), out_dtype),
        scratch_shapes=[pltpu.VMEM((tokens, width), f32), woven(step, half)],
        compiler_params=params(SMALL_VMEM),
        cost_estimate=cost(2 * rows * tokens * width, 2 * rows * width + 8 * tokens * width),
        name="collect_rows",
    )(*stay(chosen), returned, *stay(base))


def probs_kernel(q_ref, k_ref, seen_ref, out_ref):
    length = q_ref.shape[0]
    block = length // 2
    scale = HEAD_DIM ** (-0.5)
    for part in range(2):
        keys = (part + 1) * block
        cols = slice(part * block, (part + 1) * block)
        scores = lax.dot_general(
            k_ref[:keys, :], q_ref[cols, :], (((1,), (1,)), ((), ())), preferred_element_type=f32
        )
        scores = jnp.where(seen_ref[:keys, cols] > 0, scores * scale, -jnp.inf)
        peak = jnp.max(scores, axis=0, keepdims=True)
        exponent = jnp.exp(scores - peak)
        out_ref[0, :keys, cols] = exponent / jnp.sum(exponent, axis=0, keepdims=True)
        if keys < length:
            out_ref[0, keys:, cols] = jnp.zeros((length - keys, block), f32)


def attention_probs(queries, keys, seen):
    length, heads = queries.shape[0], queries.shape[1] // HEAD_DIM
    return pl.pallas_call(
        probs_kernel,
        grid=(heads,),
        in_specs=[
            pl.BlockSpec((length, HEAD_DIM), lambda h: (0, h)),
            pl.BlockSpec(keys.shape, lambda h: (0, 0)),
            pl.BlockSpec(seen.shape, lambda h: (0, 0)),
        ],
        out_specs=pl.BlockSpec((1, length, length), lambda h: (h, 0, 0)),
        out_shape=pltpu.HBM((heads, length, length), f32),
        compiler_params=params(SMALL_VMEM),
        cost_estimate=cost(
            2 * heads * length * length * HEAD_DIM,
            4 * heads * length * length,
            heads * length * length,
        ),
        name="attention_probs",
    )(queries, keys, seen)


def head_grads(probs_ref, grad_ref, q_ref, v_ref, kt_ref, out_ref, sum_k, sum_v):
    length = q_ref.shape[0]
    block = length // 2
    scale = HEAD_DIM ** (-0.5)
    for part in range(2):
        keys = (part + 1) * block
        cols = slice(part * block, (part + 1) * block)
        probs = probs_ref[0, :keys, cols]
        grad = grad_ref[cols, :]
        prob_grad = lax.dot_general(
            v_ref[:keys, :], grad, (((1,), (1,)), ((), ())), preferred_element_type=f32
        )
        row_total = jnp.sum(probs * prob_grad, axis=0, keepdims=True)
        score_grad = (probs * (prob_grad - row_total)).astype(bf16)
        query_grad = jnp.dot(kt_ref[:, :keys], score_grad, preferred_element_type=f32) * scale
        out_ref[cols, :] = query_grad.T.astype(bf16)
        sum_k[:keys, :] += jnp.dot(score_grad, q_ref[cols, :], preferred_element_type=f32)
        sum_v[:keys, :] += jnp.dot(probs.astype(bf16), grad, preferred_element_type=f32)


def first_grads_kernel(probs_ref, grad_ref, q_ref, v_ref, kt_ref, out_ref, sum_k, sum_v):
    @pl.when(pl.program_id(0) == 0)
    def _():
        sum_k[...] = jnp.zeros_like(sum_k)
        sum_v[...] = jnp.zeros_like(sum_v)

    head_grads(probs_ref, grad_ref, q_ref, v_ref, kt_ref, out_ref, sum_k, sum_v)


def last_grads_kernel(
    probs_ref, grad_ref, q_ref, v_ref, kt_ref, old_k, old_v, out_ref, sum_k, sum_v
):
    head, heads = pl.program_id(0), pl.num_programs(0)
    scale = HEAD_DIM ** (-0.5)

    @pl.when(head == 0)
    def _():
        sum_k[...] = old_k[...]
        sum_v[...] = old_v[...]

    first = pl.multiple_of((head + 2) * HEAD_DIM, HEAD_DIM)
    out_ref[:, pl.ds(first, HEAD_DIM)] = grad_ref[...]
    first = pl.multiple_of((head + heads + 2) * HEAD_DIM, HEAD_DIM)
    out = out_ref.at[:, pl.ds(first, HEAD_DIM)]
    head_grads(probs_ref, grad_ref, q_ref, v_ref, kt_ref, out, sum_k, sum_v)

    @pl.when(head == heads - 1)
    def _():
        out_ref[:, :HEAD_DIM] = (sum_k[...] * scale).astype(bf16)
        out_ref[:, HEAD_DIM : 2 * HEAD_DIM] = sum_v[...].astype(bf16)


def attention_grads(probs, out_grad, queries, values, keys_t, first, sums=None):
    length, heads = out_grad.shape[0], out_grad.shape[1] // HEAD_DIM
    whole = pl.BlockSpec((length, HEAD_DIM), lambda h: (0, 0))
    totals = [jax.ShapeDtypeStruct((length, HEAD_DIM), f32)] * 2
    out_spec = pl.BlockSpec((length, HEAD_DIM), lambda h: (0, h))
    in_specs = [
        pl.BlockSpec((1, length, length), lambda h: (first + h, 0, 0)),
        out_spec,
        pl.BlockSpec((length, HEAD_DIM), lambda h: (0, first + h)),
        whole,
        pl.BlockSpec(keys_t.shape, lambda h: (0, 0)),
    ]
    estimate = cost(8 * heads * length * length * HEAD_DIM, 4 * heads * length * length)
    operands = (*stay(probs), out_grad, *stay(queries), values, keys_t)
    if sums is None:
        return pl.pallas_call(
            first_grads_kernel,
            grid=(heads,),
            in_specs=in_specs,
            out_specs=[out_spec, whole, whole],
            out_shape=[jax.ShapeDtypeStruct(out_grad.shape, bf16)] + totals,
            compiler_params=params(SMALL_VMEM),
            cost_estimate=estimate,
            name="first_grads",
        )(*operands)
    columns = (2 * heads + 2) * HEAD_DIM
    return pl.pallas_call(
        last_grads_kernel,
        grid=(heads,),
        in_specs=in_specs + [whole, whole],
        out_specs=pl.BlockSpec((length, columns), lambda h: (0, 0)),
        out_shape=jax.ShapeDtypeStruct((length, columns), bf16),
        scratch_shapes=[pltpu.VMEM((length, HEAD_DIM), f32)] * 2,
        compiler_params=params(SMALL_VMEM),
        cost_estimate=estimate,
        name="last_grads",
    )(*operands, *sums)


def pass_round(pieces):
    parts = lax.axis_size("cp")
    me = lax.axis_index("cp")
    got = []
    for shift in range(parts):
        piece = pieces((me + shift) % parts)
        if shift:
            piece = lax.ppermute(piece, "cp", [(i, (i + shift) % parts) for i in range(parts)])
        got.append((piece, (me - shift) % parts))
    return got


def to_heads(queries):
    parts = lax.axis_size("cp")
    rows, width = queries.shape[0], queries.shape[1] // parts
    out = jnp.zeros((parts * rows, width), queries.dtype)
    for piece, i in pass_round(lambda i: lax.dynamic_slice_in_dim(queries, i * width, width, 1)):
        out = lax.dynamic_update_slice(out, piece, (i * rows, 0))
    return out


def to_rows(grads):
    rows = grads.shape[0] // lax.axis_size("cp")
    return pass_round(lambda i: lax.dynamic_slice_in_dim(grads, i * rows, rows, 0))


def join_rows(pieces, most, width):
    rows = pieces[0][0].shape[0]
    out = jnp.zeros((rows, len(pieces) * width), bf16)
    for piece, i in pieces:
        out = lax.dynamic_update_slice(out, piece, (0, i * width))
    return out


def finish_kernel(last, together, got_ref, *refs):
    grad_ref, query_ref, key_ref, value_ref, sum_k, sum_v = refs[2:]
    place = pl.program_id(0) % together
    key = got_ref[0, :, :HEAD_DIM].astype(f32)
    value = got_ref[0, :, HEAD_DIM : 2 * HEAD_DIM].astype(f32)
    grad_ref[...] = got_ref[0, :, 2 * HEAD_DIM : 2 * HEAD_DIM + last]
    query_ref[...] = got_ref[0, :, 2 * HEAD_DIM + last :]

    @pl.when(place == 0)
    def _():
        sum_k[...] = key
        sum_v[...] = value

    @pl.when(place > 0)
    def _():
        sum_k[...] += key
        sum_v[...] += value

    key_ref[...] = sum_k[...].astype(bf16)
    value_ref[...] = sum_v[...].astype(bf16)


def finish(got, grad_hidden, grad_query, together):
    parts, rows, columns = got.shape
    last = (columns - 2 * HEAD_DIM) // 2
    ratio = grad_hidden.shape[1] // parts // last
    rest = pl.BlockSpec((rows, last), lambda i: (0, i * ratio + ratio - 1))
    sums = pl.BlockSpec((rows, HEAD_DIM), lambda i: (0, i // together))
    sums_shape = jax.ShapeDtypeStruct((rows, parts // together * HEAD_DIM), bf16)
    return pl.pallas_call(
        functools.partial(finish_kernel, last, together),
        grid=(parts,),
        in_specs=[
            pl.BlockSpec((1, rows, columns), lambda i: (i, 0, 0)),
            pl.BlockSpec(memory_space=pl.ANY),
            pl.BlockSpec(memory_space=pl.ANY),
        ],
        out_specs=[rest, rest, sums, sums],
        out_shape=[
            jax.ShapeDtypeStruct(grad_hidden.shape, bf16),
            jax.ShapeDtypeStruct(grad_query.shape, bf16),
            sums_shape,
            sums_shape,
        ],
        input_output_aliases={1: 0, 2: 1},
        scratch_shapes=[pltpu.VMEM((rows, HEAD_DIM), f32)] * 2,
        compiler_params=params(SMALL_VMEM),
        cost_estimate=cost(4 * got.size, 4 * got.size),
        name="finish",
    )(got, grad_hidden, grad_query)


def seen_keys(mask_table, length):
    blocks = mask_table.shape[0]
    size = length // blocks
    pos = jnp.arange(length, dtype=jnp.int32)
    near = jnp.broadcast_to(mask_table.T[:, None, :, None], (blocks, size, blocks, size))
    near = near.reshape(length, length) > 0
    same = (pos // size)[:, None] == (pos // size)[None, :]
    return ((pos[:, None] <= pos[None, :]) & (same | near)).astype(f32)


def swap(rows, axis):
    return lax.all_to_all(rows, axis, split_axis=0, concat_axis=0, tiled=True)


def on_device(
    grad_out,
    route_ids,
    fallback_ids,
    slot_ids,
    route_probs,
    w_gate,
    w_up,
    w_down,
    gate_pre,
    up_pre,
    queries,
    key_vectors,
    value_vectors,
    block_mask,
):
    experts = lax.axis_size("ep")
    quarters = lax.axis_size("cp")
    tokens, width = grad_out.shape
    slot_count = gate_pre.shape[2]
    capacity = slot_count // experts
    share = capacity // PARTS
    part_rows = experts * share
    half = width // 2

    routes = (route_ids.T, fallback_ids.T, slot_ids.T)
    probs_t = route_probs.T
    outgoing = [
        send_rows(part, experts, capacity, *routes, probs_t, grad_out) for part in range(PARTS)
    ]
    saved = lax.all_gather(jnp.stack([gate_pre[0], up_pre[0]]), "cp", axis=0)

    overflow = routes[2] >= capacity
    expert = jnp.where(overflow, routes[1], routes[0])
    slot = routes[2] - jnp.where(overflow, capacity, 0)
    in_part = [
        jnp.where(slot // share == part, expert * share + slot - part * share, -1).T
        for part in range(PARTS)
    ]
    my_queries = to_heads(queries)
    heads_here = width // HEAD_DIM
    group = heads_here * quarters // (key_vectors.shape[1] // HEAD_DIM)
    kv_head = lax.axis_index("cp") * heads_here // group
    keys = lax.dynamic_slice_in_dim(key_vectors, kv_head * HEAD_DIM, HEAD_DIM, 1)
    values = lax.dynamic_slice_in_dim(value_vectors, kv_head * HEAD_DIM, HEAD_DIM, 1)
    probs = attention_probs(my_queries, keys, seen_keys(block_mask[0], tokens))
    early = lax.optimization_barrier((outgoing[1], turn_weights(w_down[0]), in_part))
    outgoing[1], down_t, in_part = early

    def exchange(rows):
        wide = rows.shape[1]
        rows = swap(rows.reshape(experts, 2 * share, wide), "ep")
        return rows.reshape(2 * part_rows, wide)

    arrived = exchange(outgoing[0])
    first_sum, rows = lax.optimization_barrier((project_down(arrived, down_t), outgoing[1]))
    hidden_grad = lax.psum(first_sum, "cp")
    arrived = exchange(rows)
    saved = turn_saved(saved, share)
    (rows,) = expert_rows(hidden_grad, saved[0], saved[1], w_gate[0], w_up[0], [width])
    arrived, rows, saved = lax.optimization_barrier((arrived, rows, saved))
    later_sum = project_down(arrived, down_t)
    rows, _ = lax.optimization_barrier((rows, later_sum))
    back = [list(range(quarters))[::-1]]
    later_grad = lax.psum(later_sum, "cp", axis_index_groups=back)
    returned = exchange(rows)
    last = width // LAST_SHARE
    most = width - last
    rows = expert_rows(later_grad, saved[2], saved[3], w_gate[0], w_up[0], [most, last])
    returned_most = exchange(rows[0])
    chosen = [chosen_rows(slots, part_rows) for slots in in_part]
    total = collect_rows(chosen[0], *stay(returned), grad_out, 0, f32)
    ready = (returned_most, rows[1], chosen, total, probs, my_queries, values, keys.T)
    ready = lax.optimization_barrier(ready)
    returned_most, last_rows, chosen, total, probs, my_queries, values, keys_t = ready
    returned_last = exchange(last_rows)

    most_grad = collect_rows(chosen[1], returned_most, total, 0, bf16)
    grad_pieces = to_rows(most_grad)
    query_part, *sums = attention_grads(probs, most_grad, my_queries, values, keys_t, 0)
    query_pieces = to_rows(query_part)

    last_grad = collect_rows(chosen[1], returned_last, total, most, bf16)
    packed = attention_grads(
        probs, last_grad, my_queries, values, keys_t, most // HEAD_DIM, sums
    )
    ready = (packed, [p for p, _ in grad_pieces], [p for p, _ in query_pieces])
    packed, grads, query_grads = lax.optimization_barrier(ready)
    rows_here = tokens // quarters
    packed = swap(packed.reshape(quarters, rows_here, -1), "cp")
    grad_hidden = join_rows([(p, i) for p, (_, i) in zip(grads, grad_pieces)], most, width)
    grad_query = join_rows([(p, i) for p, (_, i) in zip(query_grads, query_pieces)], most, width)
    return finish(packed, grad_hidden, grad_query, group // heads_here)


def solution(mesh):
    in_specs = (
        P("ep", "cp"),
        P("ep", None),
        P("ep", None),
        P("ep", None),
        P("ep", None),
        P("ep", None, "cp"),
        P("ep", None, "cp"),
        P("ep", None, "cp"),
        P("ep", "cp", None),
        P("ep", "cp", None),
        P(("ep", "cp"), None),
        P("ep", None),
        P("ep", None),
        P("ep", None, None),
    )
    out_specs = (
        P(("ep", "cp"), None),
        P(("ep", "cp"), None),
        P(("ep", "cp"), None),
        P(("ep", "cp"), None),
    )
    return jax.shard_map(
        on_device, mesh=mesh, in_specs=in_specs, out_specs=out_specs, check_vma=False
    )
```

```python
import functools

import jax
import jax.numpy as jnp
from jax import lax
from jax.experimental import pallas as pl
from jax.experimental.pallas import tpu as pltpu
from jax.sharding import PartitionSpec as P

HEAD_DIM = 128
LANES = 128
PARTS = 2
STEPS = 4
CHOSEN_STEPS = 2
DOWN_STEPS = 3
DOWN_COLS = 256
PROJECT_STEPS = 2
LAST_SHARE = 4
VMEM_LIMIT = 56 * 1024 * 1024
SMALL_VMEM = 24 * 1024 * 1024

f32 = jnp.float32
bf16 = jnp.bfloat16


def params(limit=VMEM_LIMIT):
    return pltpu.CompilerParams(vmem_limit_bytes=limit)


def stay(*arrays):
    return [pltpu.with_memory_space_constraint(a, pltpu.HBM) for a in arrays]


def cost(flops, moved, exps=0):
    return pl.CostEstimate(flops=flops, bytes_accessed=moved, transcendentals=exps)


def weave(out_ref, wide, low, high):
    rows = low.shape[0]
    for j in range(wide.shape[0]):
        cols = slice(j * LANES, (j + 1) * LANES)
        wide[j, pl.ds(0, rows, 2), :] = low[:, cols]
        wide[j, pl.ds(1, rows, 2), :] = high[:, cols]
        out_ref[:, cols] = wide[j, : 2 * rows, :].astype(bf16)


def unweave(rows_ref, wide):
    slabs, rows = wide.shape[0], rows_ref.shape[0] // 2
    for j in range(slabs):
        wide[j, : 2 * rows, :] = rows_ref[:, j * LANES : (j + 1) * LANES].astype(f32)
    low = [wide[j, pl.ds(0, rows, 2), :].astype(bf16) for j in range(slabs)]
    high = [wide[j, pl.ds(1, rows, 2), :].astype(bf16) for j in range(slabs)]
    return jnp.concatenate(low, axis=1), jnp.concatenate(high, axis=1)


def woven(rows, half):
    return pltpu.VMEM((half // LANES, 2 * rows + 8, LANES), f32)


def split_by(row, size, count):
    factor = (1 << 16) // size + 1
    assert all((r * factor) >> 16 == r // size for r in range(count))
    return (row * factor) >> 16


def route_rows(part, capacity, ids_ref, spare_ref, slot_ref, probs_ref, grad_ref, out_ref, wide):
    rows, half = out_ref.shape[0] // 2, out_ref.shape[1]
    tokens = grad_ref.shape[0]
    share = capacity // PARTS
    overflow = slot_ref[...] >= capacity
    expert = jnp.where(overflow, spare_ref[...], ids_ref[...])
    target = expert * capacity + slot_ref[...] - jnp.where(overflow, capacity, 0)
    row = lax.broadcasted_iota(jnp.int32, (rows, 1), 0) + pl.program_id(0) * rows
    group = split_by(row, share, rows * STEPS)
    dest = group * (capacity - share) + row + part * share
    weights = jnp.zeros((rows, tokens), f32)
    for k in range(target.shape[0]):
        weights = jnp.where(target[k : k + 1, :] == dest, probs_ref[k : k + 1, :], weights)
    weight = jnp.sum(weights, axis=1, keepdims=True)
    chosen = jnp.where(weights != 0.0, 1.0, 0.0).astype(bf16)
    picked = jnp.dot(chosen, grad_ref[...], preferred_element_type=f32)
    picked = picked * weight
    weave(out_ref, wide, picked[:, :half], picked[:, half:])


def send_rows(part, experts, capacity, ids, spare, slots, probs, grad):
    rows, (tokens, width) = experts * capacity // PARTS, grad.shape
    step, half = rows // STEPS, width // 2
    routes = pl.BlockSpec(slots.shape, lambda i: (0, 0))
    return pl.pallas_call(
        functools.partial(route_rows, part, capacity),
        grid=(STEPS,),
        in_specs=[routes] * 4 + [pl.BlockSpec(grad.shape, lambda i: (0, 0))],
        out_specs=pl.BlockSpec((2 * step, half), lambda i: (i, 0)),
        out_shape=pltpu.HBM((2 * rows, half), bf16),
        scratch_shapes=[woven(step, half)],
        compiler_params=params(),
        cost_estimate=cost(2 * rows * tokens * width, 4 * rows * width),
        name="send_rows",
    )(ids, spare, slots, probs, *stay(grad))


def turn_kernel(share, saved_ref, *refs):
    outs, tall = refs[:-1], refs[-1]
    quarters, kinds = saved_ref.shape[:2]
    groups = saved_ref.shape[3] // (PARTS * share)
    for kind in range(kinds):
        hidden = jnp.concatenate([saved_ref[c, kind] for c in range(quarters)], axis=0)
        rows = hidden.astype(f32).T
        for part in range(PARTS):
            for g in range(groups):
                start = (g * PARTS + part) * share
                tall[g * share : (g + 1) * share, :] = rows[start : start + share, :]
            outs[part * kinds + kind][...] = tall[...].astype(bf16)


def turn_saved(saved, share):
    quarters, kinds, units, slots = saved.shape
    hidden, rows = quarters * units, slots // PARTS
    step = rows // STEPS
    return pl.pallas_call(
        functools.partial(turn_kernel, share),
        grid=(STEPS,),
        in_specs=[pl.BlockSpec((quarters, kinds, units, PARTS * step), lambda i: (0, 0, 0, i))],
        out_specs=[pl.BlockSpec((step, hidden), lambda i: (i, 0))] * (PARTS * kinds),
        out_shape=[jax.ShapeDtypeStruct((rows, hidden), bf16)] * (PARTS * kinds),
        scratch_shapes=[pltpu.VMEM((step, hidden), f32)],
        compiler_params=params(),
        cost_estimate=cost(saved.size, 4 * saved.size),
        name="turn_saved",
    )(saved)


def turn_kernel_2d(in_ref, out_ref):
    out_ref[...] = in_ref[...].astype(f32).T.astype(bf16)


def turn_weights(weights):
    hidden, width = weights.shape
    step = hidden // DOWN_STEPS
    return pl.pallas_call(
        turn_kernel_2d,
        grid=(DOWN_STEPS,),
        in_specs=[pl.BlockSpec((step, width), lambda i: (i, 0))],
        out_specs=pl.BlockSpec((width, step), lambda i: (0, i)),
        out_shape=pltpu.HBM((width, hidden), bf16),
        compiler_params=params(SMALL_VMEM),
        cost_estimate=cost(weights.size, 4 * weights.size),
        name="turn_weights",
    )(*stay(weights))


def down_rows_kernel(rows_ref, low_ref, high_ref, out_ref, wide):
    low, high = unweave(rows_ref, wide)
    for start in range(0, out_ref.shape[1], DOWN_COLS):
        cols = slice(start, start + DOWN_COLS)
        total = jnp.dot(low, low_ref[:, cols], preferred_element_type=f32)
        total = total + jnp.dot(high, high_ref[:, cols], preferred_element_type=f32)
        out_ref[:, cols] = total.astype(bf16)


def project_down(arrived, down_t):
    rows, half = arrived.shape[0] // 2, arrived.shape[1]
    width, hidden = down_t.shape
    step = rows // PROJECT_STEPS
    return pl.pallas_call(
        down_rows_kernel,
        grid=(PROJECT_STEPS,),
        in_specs=[
            pl.BlockSpec((2 * step, half), lambda i: (i, 0)),
            pl.BlockSpec((half, hidden), lambda i: (0, 0)),
            pl.BlockSpec((half, hidden), lambda i: (1, 0)),
        ],
        out_specs=pl.BlockSpec((step, hidden), lambda i: (i, 0)),
        out_shape=pltpu.HBM((rows, hidden), bf16),
        scratch_shapes=[woven(step, half)],
        compiler_params=params(SMALL_VMEM),
        cost_estimate=cost(2 * rows * width * hidden, 2 * rows * (width + hidden)),
        name="project_down",
    )(arrived, *stay(down_t, down_t))


def expert_kernel(hidden_ref, gate_ref, up_ref, *refs):
    weights, refs = refs[:4], refs[4:]
    outs, wides = refs[: len(refs) // 2], refs[len(refs) // 2 :]
    grad = hidden_ref[...].astype(f32)
    gate = gate_ref[...].astype(f32)
    up = up_ref[...].astype(f32)
    sig = 1.0 / (1.0 + jnp.exp(-gate))
    shared = grad * sig
    gate_grad = (shared * up * (1.0 + gate * (1.0 - sig))).astype(bf16)
    up_grad = (shared * gate).astype(bf16)
    halves = [
        jnp.dot(gate_grad, wg_ref[...], preferred_element_type=f32)
        + jnp.dot(up_grad, wu_ref[...], preferred_element_type=f32)
        for wg_ref, wu_ref in (weights[:2], weights[2:])
    ]
    total = jnp.concatenate(halves, axis=1)
    start = 0
    for out_ref, wide in zip(outs, wides):
        half = out_ref.shape[1]
        low, high = total[:, start : start + half], total[:, start + half : start + 2 * half]
        weave(out_ref, wide, low, high)
        start += 2 * half


def expert_rows(hidden_grad, gate, up, w_gate, w_up, widths):
    rows, hidden = hidden_grad.shape
    step, width = rows // STEPS, sum(widths)
    row_block = pl.BlockSpec((step, hidden), lambda i: (i, 0))
    halves = [pl.BlockSpec((hidden, width // 2), lambda i, j=j: (0, j)) for j in (0, 0, 1, 1)]
    return pl.pallas_call(
        expert_kernel,
        grid=(STEPS,),
        in_specs=[row_block, row_block, row_block] + halves,
        out_specs=[pl.BlockSpec((2 * step, w // 2), lambda i: (i, 0)) for w in widths],
        out_shape=[jax.ShapeDtypeStruct((2 * rows, w // 2), bf16) for w in widths],
        scratch_shapes=[woven(step, w // 2) for w in widths],
        compiler_params=params(),
        cost_estimate=cost(
            128 * rows * hidden * width, 2 * rows * (3 * hidden + width), rows * hidden
        ),
        name="expert_rows",
    )(hidden_grad, gate, up, w_gate, w_up, w_gate, w_up)


def chosen_kernel(slots_ref, out_ref):
    tokens, rows = out_ref.shape
    row = lax.broadcasted_iota(jnp.int32, (tokens, rows), 1) + pl.program_id(0) * rows
    chosen = jnp.zeros((tokens, rows), f32)
    for k in range(slots_ref.shape[1]):
        chosen = jnp.where(slots_ref[:, k : k + 1] == row, 1.0, chosen)
    out_ref[...] = chosen.astype(bf16)


def chosen_rows(slots, rows):
    tokens = slots.shape[0]
    step = rows // CHOSEN_STEPS
    return pl.pallas_call(
        chosen_kernel,
        grid=(CHOSEN_STEPS,),
        in_specs=[pl.BlockSpec(slots.shape, lambda i: (0, 0))],
        out_specs=pl.BlockSpec((tokens, step), lambda i: (0, i)),
        out_shape=pltpu.HBM((tokens, rows), bf16),
        compiler_params=params(SMALL_VMEM),
        cost_estimate=cost(8 * tokens * rows, 2 * tokens * rows),
        name="chosen_rows",
    )(slots)


def collect_kernel(chosen_ref, rows_ref, base_ref, out_ref, total, wide):
    step = pl.program_id(0)
    half = rows_ref.shape[1]

    @pl.when(step == 0)
    def _():
        total[...] = base_ref[...].astype(f32)

    low, high = unweave(rows_ref, wide)
    total[:, :half] += jnp.dot(chosen_ref[...], low, preferred_element_type=f32)
    total[:, half:] += jnp.dot(chosen_ref[...], high, preferred_element_type=f32)

    @pl.when(step == CHOSEN_STEPS - 1)
    def _():
        out_ref[...] = total[...].astype(out_ref.dtype)


def collect_rows(chosen, returned, base, start, out_dtype):
    rows, half = returned.shape[0] // 2, returned.shape[1]
    tokens, width = base.shape[0], 2 * half
    step, column = rows // CHOSEN_STEPS, start // width
    assert column * width == start
    return pl.pallas_call(
        collect_kernel,
        grid=(CHOSEN_STEPS,),
        in_specs=[
            pl.BlockSpec((tokens, step), lambda i: (0, i)),
            pl.BlockSpec((2 * step, half), lambda i: (i, 0)),
            pl.BlockSpec((tokens, width), lambda i: (0, column)),
        ],
        out_specs=pl.BlockSpec((tokens, width), lambda i: (0, 0)),
        out_shape=jax.ShapeDtypeStruct((tokens, width), out_dtype),
        scratch_shapes=[pltpu.VMEM((tokens, width), f32), woven(step, half)],
        compiler_params=params(SMALL_VMEM),
        cost_estimate=cost(2 * rows * tokens * width, 2 * rows * width + 8 * tokens * width),
        name="collect_rows",
    )(*stay(chosen), returned, *stay(base))


def probs_kernel(q_ref, k_ref, seen_ref, out_ref):
    length = q_ref.shape[0]
    block = length // 2
    scale = HEAD_DIM ** (-0.5)
    for part in range(2):
        keys = (part + 1) * block
        cols = slice(part * block, (part + 1) * block)
        scores = lax.dot_general(
            k_ref[:keys, :], q_ref[cols, :], (((1,), (1,)), ((), ())), preferred_element_type=f32
        )
        scores = jnp.where(seen_ref[:keys, cols] > 0, scores * scale, -jnp.inf)
        peak = jnp.max(scores, axis=0, keepdims=True)
        exponent = jnp.exp(scores - peak)
        out_ref[0, :keys, cols] = exponent / jnp.sum(exponent, axis=0, keepdims=True)
        if keys < length:
            out_ref[0, keys:, cols] = jnp.zeros((length - keys, block), f32)


def attention_probs(queries, keys, seen):
    length, heads = queries.shape[0], queries.shape[1] // HEAD_DIM
    return pl.pallas_call(
        probs_kernel,
        grid=(heads,),
        in_specs=[
            pl.BlockSpec((length, HEAD_DIM), lambda h: (0, h)),
            pl.BlockSpec(keys.shape, lambda h: (0, 0)),
            pl.BlockSpec(seen.shape, lambda h: (0, 0)),
        ],
        out_specs=pl.BlockSpec((1, length, length), lambda h: (h, 0, 0)),
        out_shape=pltpu.HBM((heads, length, length), f32),
        compiler_params=params(SMALL_VMEM),
        cost_estimate=cost(
            2 * heads * length * length * HEAD_DIM,
            4 * heads * length * length,
            heads * length * length,
        ),
        name="attention_probs",
    )(queries, keys, seen)


def head_grads(probs_refs, grad_ref, q_ref, v_ref, kt_ref, out_ref, sum_k, sum_v):
    length = q_ref.shape[0]
    block = length // 2
    scale = HEAD_DIM ** (-0.5)
    for part in range(2):
        keys = (part + 1) * block
        cols = slice(part * block, (part + 1) * block)
        probs = probs_refs[part][0]
        grad = grad_ref[cols, :]
        prob_grad = lax.dot_general(
            v_ref[:keys, :], grad, (((1,), (1,)), ((), ())), preferred_element_type=f32
        )
        row_total = jnp.sum(probs * prob_grad, axis=0, keepdims=True)
        score_grad = (probs * (prob_grad - row_total)).astype(bf16)
        query_grad = jnp.dot(kt_ref[:, :keys], score_grad, preferred_element_type=f32) * scale
        out_ref[cols, :] = query_grad.T.astype(bf16)
        sum_k[:keys, :] += jnp.dot(score_grad, q_ref[cols, :], preferred_element_type=f32)
        sum_v[:keys, :] += jnp.dot(probs.astype(bf16), grad, preferred_element_type=f32)


def first_grads_kernel(
    early_ref, late_ref, grad_ref, q_ref, v_ref, kt_ref, out_ref, sum_k, sum_v
):
    @pl.when(pl.program_id(0) == 0)
    def _():
        sum_k[...] = jnp.zeros_like(sum_k)
        sum_v[...] = jnp.zeros_like(sum_v)

    head_grads((early_ref, late_ref), grad_ref, q_ref, v_ref, kt_ref, out_ref, sum_k, sum_v)


def last_grads_kernel(
    early_ref, late_ref, grad_ref, q_ref, v_ref, kt_ref, old_k, old_v, out_ref, sum_k, sum_v
):
    head, heads = pl.program_id(0), pl.num_programs(0)
    scale = HEAD_DIM ** (-0.5)

    @pl.when(head == 0)
    def _():
        sum_k[...] = old_k[...]
        sum_v[...] = old_v[...]

    first = pl.multiple_of((head + 2) * HEAD_DIM, HEAD_DIM)
    out_ref[:, pl.ds(first, HEAD_DIM)] = grad_ref[...]
    first = pl.multiple_of((head + heads + 2) * HEAD_DIM, HEAD_DIM)
    out = out_ref.at[:, pl.ds(first, HEAD_DIM)]
    head_grads((early_ref, late_ref), grad_ref, q_ref, v_ref, kt_ref, out, sum_k, sum_v)

    @pl.when(head == heads - 1)
    def _():
        out_ref[:, :HEAD_DIM] = (sum_k[...] * scale).astype(bf16)
        out_ref[:, HEAD_DIM : 2 * HEAD_DIM] = sum_v[...].astype(bf16)


def attention_grads(probs, out_grad, queries, values, keys_t, first, sums=None):
    length, heads = out_grad.shape[0], out_grad.shape[1] // HEAD_DIM
    whole = pl.BlockSpec((length, HEAD_DIM), lambda h: (0, 0))
    totals = [jax.ShapeDtypeStruct((length, HEAD_DIM), f32)] * 2
    out_spec = pl.BlockSpec((length, HEAD_DIM), lambda h: (0, h))
    in_specs = [
        pl.BlockSpec((1, length // 2, length // 2), lambda h: (first + h, 0, 0)),
        pl.BlockSpec((1, length, length // 2), lambda h: (first + h, 0, 1)),
        out_spec,
        pl.BlockSpec((length, HEAD_DIM), lambda h: (0, first + h)),
        whole,
        pl.BlockSpec(keys_t.shape, lambda h: (0, 0)),
    ]
    estimate = cost(8 * heads * length * length * HEAD_DIM, 4 * heads * length * length)
    operands = (*stay(probs, probs), out_grad, *stay(queries), values, keys_t)
    if sums is None:
        return pl.pallas_call(
            first_grads_kernel,
            grid=(heads,),
            in_specs=in_specs,
            out_specs=[out_spec, whole, whole],
            out_shape=[jax.ShapeDtypeStruct(out_grad.shape, bf16)] + totals,
            compiler_params=params(SMALL_VMEM),
            cost_estimate=estimate,
            name="first_grads",
        )(*operands)
    columns = (2 * heads + 2) * HEAD_DIM
    return pl.pallas_call(
        last_grads_kernel,
        grid=(heads,),
        in_specs=in_specs + [whole, whole],
        out_specs=pl.BlockSpec((length, columns), lambda h: (0, 0)),
        out_shape=jax.ShapeDtypeStruct((length, columns), bf16),
        scratch_shapes=[pltpu.VMEM((length, HEAD_DIM), f32)] * 2,
        compiler_params=params(SMALL_VMEM),
        cost_estimate=estimate,
        name="last_grads",
    )(*operands, *sums)


def pass_round(pieces):
    parts = lax.axis_size("cp")
    me = lax.axis_index("cp")
    got = []
    for shift in range(parts):
        piece = pieces((me + shift) % parts)
        if shift:
            piece = lax.ppermute(piece, "cp", [(i, (i + shift) % parts) for i in range(parts)])
        got.append((piece, (me - shift) % parts))
    return got


def to_heads(queries):
    parts = lax.axis_size("cp")
    rows, width = queries.shape[0], queries.shape[1] // parts
    out = jnp.zeros((parts * rows, width), queries.dtype)
    for piece, i in pass_round(lambda i: lax.dynamic_slice_in_dim(queries, i * width, width, 1)):
        out = lax.dynamic_update_slice(out, piece, (i * rows, 0))
    return out


def to_rows(grads):
    rows = grads.shape[0] // lax.axis_size("cp")
    return pass_round(lambda i: lax.dynamic_slice_in_dim(grads, i * rows, rows, 0))


def join_rows(pieces, most, width):
    rows = pieces[0][0].shape[0]
    out = jnp.zeros((rows, len(pieces) * width), bf16)
    for piece, i in pieces:
        out = lax.dynamic_update_slice(out, piece, (0, i * width))
    return out


def finish_kernel(last, together, got_ref, *refs):
    grad_ref, query_ref, key_ref, value_ref, sum_k, sum_v = refs[2:]
    place = pl.program_id(0) % together
    key = got_ref[0, :, :HEAD_DIM].astype(f32)
    value = got_ref[0, :, HEAD_DIM : 2 * HEAD_DIM].astype(f32)
    grad_ref[...] = got_ref[0, :, 2 * HEAD_DIM : 2 * HEAD_DIM + last]
    query_ref[...] = got_ref[0, :, 2 * HEAD_DIM + last :]

    @pl.when(place == 0)
    def _():
        sum_k[...] = key
        sum_v[...] = value

    @pl.when(place > 0)
    def _():
        sum_k[...] += key
        sum_v[...] += value

    key_ref[...] = sum_k[...].astype(bf16)
    value_ref[...] = sum_v[...].astype(bf16)


def finish(got, grad_hidden, grad_query, together):
    parts, rows, columns = got.shape
    last = (columns - 2 * HEAD_DIM) // 2
    ratio = grad_hidden.shape[1] // parts // last
    rest = pl.BlockSpec((rows, last), lambda i: (0, i * ratio + ratio - 1))
    sums = pl.BlockSpec((rows, HEAD_DIM), lambda i: (0, i // together))
    sums_shape = jax.ShapeDtypeStruct((rows, parts // together * HEAD_DIM), bf16)
    return pl.pallas_call(
        functools.partial(finish_kernel, last, together),
        grid=(parts,),
        in_specs=[
            pl.BlockSpec((1, rows, columns), lambda i: (i, 0, 0)),
            pl.BlockSpec(memory_space=pl.ANY),
            pl.BlockSpec(memory_space=pl.ANY),
        ],
        out_specs=[rest, rest, sums, sums],
        out_shape=[
            jax.ShapeDtypeStruct(grad_hidden.shape, bf16),
            jax.ShapeDtypeStruct(grad_query.shape, bf16),
            sums_shape,
            sums_shape,
        ],
        input_output_aliases={1: 0, 2: 1},
        scratch_shapes=[pltpu.VMEM((rows, HEAD_DIM), f32)] * 2,
        compiler_params=params(SMALL_VMEM),
        cost_estimate=cost(4 * got.size, 4 * got.size),
        name="finish",
    )(got, grad_hidden, grad_query)


def seen_keys(mask_table, length):
    blocks = mask_table.shape[0]
    size = length // blocks
    pos = jnp.arange(length, dtype=jnp.int32)
    near = jnp.broadcast_to(mask_table.T[:, None, :, None], (blocks, size, blocks, size))
    near = near.reshape(length, length) > 0
    same = (pos // size)[:, None] == (pos // size)[None, :]
    return ((pos[:, None] <= pos[None, :]) & (same | near)).astype(f32)


def swap(rows, axis):
    return lax.all_to_all(rows, axis, split_axis=0, concat_axis=0, tiled=True)


def on_device(
    grad_out,
    route_ids,
    fallback_ids,
    slot_ids,
    route_probs,
    w_gate,
    w_up,
    w_down,
    gate_pre,
    up_pre,
    queries,
    key_vectors,
    value_vectors,
    block_mask,
):
    experts = lax.axis_size("ep")
    quarters = lax.axis_size("cp")
    tokens, width = grad_out.shape
    slot_count = gate_pre.shape[2]
    capacity = slot_count // experts
    share = capacity // PARTS
    part_rows = experts * share
    half = width // 2

    routes = (route_ids.T, fallback_ids.T, slot_ids.T)
    probs_t = route_probs.T
    outgoing = [
        send_rows(part, experts, capacity, *routes, probs_t, grad_out) for part in range(PARTS)
    ]
    saved = lax.all_gather(jnp.stack([gate_pre[0], up_pre[0]]), "cp", axis=0)

    overflow = routes[2] >= capacity
    expert = jnp.where(overflow, routes[1], routes[0])
    slot = routes[2] - jnp.where(overflow, capacity, 0)
    in_part = [
        jnp.where(slot // share == part, expert * share + slot - part * share, -1).T
        for part in range(PARTS)
    ]
    my_queries = to_heads(queries)
    heads_here = width // HEAD_DIM
    group = heads_here * quarters // (key_vectors.shape[1] // HEAD_DIM)
    kv_head = lax.axis_index("cp") * heads_here // group
    keys = lax.dynamic_slice_in_dim(key_vectors, kv_head * HEAD_DIM, HEAD_DIM, 1)
    values = lax.dynamic_slice_in_dim(value_vectors, kv_head * HEAD_DIM, HEAD_DIM, 1)
    probs = attention_probs(my_queries, keys, seen_keys(block_mask[0], tokens))
    early = lax.optimization_barrier((outgoing[1], turn_weights(w_down[0]), in_part))
    outgoing[1], down_t, in_part = early

    def exchange(rows):
        wide = rows.shape[1]
        rows = swap(rows.reshape(experts, 2 * share, wide), "ep")
        return rows.reshape(2 * part_rows, wide)

    arrived = exchange(outgoing[0])
    first_sum, rows = lax.optimization_barrier((project_down(arrived, down_t), outgoing[1]))
    hidden_grad = lax.psum(first_sum, "cp")
    arrived = exchange(rows)
    saved = turn_saved(saved, share)
    (rows,) = expert_rows(hidden_grad, saved[0], saved[1], w_gate[0], w_up[0], [width])
    arrived, rows, saved = lax.optimization_barrier((arrived, rows, saved))
    later_sum = project_down(arrived, down_t)
    rows, _ = lax.optimization_barrier((rows, later_sum))
    back = [list(range(quarters))[::-1]]
    later_grad = lax.psum(later_sum, "cp", axis_index_groups=back)
    returned = exchange(rows)
    last = width // LAST_SHARE
    most = width - last
    rows = expert_rows(later_grad, saved[2], saved[3], w_gate[0], w_up[0], [most, last])
    returned_most = exchange(rows[0])
    chosen = [chosen_rows(slots, part_rows) for slots in in_part]
    total = collect_rows(chosen[0], *stay(returned), grad_out, 0, f32)
    ready = (returned_most, rows[1], chosen, total, probs, my_queries, values, keys.T)
    ready = lax.optimization_barrier(ready)
    returned_most, last_rows, chosen, total, probs, my_queries, values, keys_t = ready
    returned_last = exchange(last_rows)

    most_grad = collect_rows(chosen[1], returned_most, total, 0, bf16)
    grad_pieces = to_rows(most_grad)
    query_part, *sums = attention_grads(probs, most_grad, my_queries, values, keys_t, 0)
    query_pieces = to_rows(query_part)

    last_grad = collect_rows(chosen[1], returned_last, total, most, bf16)
    packed = attention_grads(
        probs, last_grad, my_queries, values, keys_t, most // HEAD_DIM, sums
    )
    ready = (packed, [p for p, _ in grad_pieces], [p for p, _ in query_pieces])
    packed, grads, query_grads = lax.optimization_barrier(ready)
    rows_here = tokens // quarters
    packed = swap(packed.reshape(quarters, rows_here, -1), "cp")
    grad_hidden = join_rows([(p, i) for p, (_, i) in zip(grads, grad_pieces)], most, width)
    grad_query = join_rows([(p, i) for p, (_, i) in zip(query_grads, query_pieces)], most, width)
    return finish(packed, grad_hidden, grad_query, group // heads_here)


def solution(mesh):
    in_specs = (
        P("ep", "cp"),
        P("ep", None),
        P("ep", None),
        P("ep", None),
        P("ep", None),
        P("ep", None, "cp"),
        P("ep", None, "cp"),
        P("ep", None, "cp"),
        P("ep", "cp", None),
        P("ep", "cp", None),
        P(("ep", "cp"), None),
        P("ep", None),
        P("ep", None),
        P("ep", None, None),
    )
    out_specs = (
        P(("ep", "cp"), None),
        P(("ep", "cp"), None),
        P(("ep", "cp"), None),
        P(("ep", "cp"), None),
    )
    return jax.shard_map(
        on_device, mesh=mesh, in_specs=in_specs, out_specs=out_specs, check_vma=False
    )
```
